32 devices in a mesh: dp: 16 (over z, y, x), tensor: 2 (over core).
Axes of the slice: x: 2, y: 2, z: 4, core: 2. Of those that a mesh axis runs over, the one named last changes fastest.
Arguments:
- tokens: bfloat16 [12288, 2048], P('dp'), may hold values from -6 to 6
- segment_ids: int32 [12288], P('dp'), may hold values from 0 to 12287, as said below
- cotangent: bfloat16 [12288, 2048], P('dp'), may hold values from -6 to 6
- mixer_gain: bfloat16 [2048], replicated, may hold values from 0.5 to 1.5
- w_query: bfloat16 [2048, 1024], P('dp', 'tensor'), as said below
- w_key: bfloat16 [2048, 1024], P('dp', 'tensor'), as said below
- w_value: bfloat16 [2048, 2048], P('dp', 'tensor'), may hold values from -0.125 to 0.125
- w_swish: bfloat16 [2048, 2048], P('dp', 'tensor'), may hold values from -0.125 to 0.125
- decay_down: bfloat16 [2048, 16], replicated, may hold values from -0.125 to 0.125
- decay_up: bfloat16 [16, 1024], replicated, may hold values from -1.5 to 1.5
- decay_bias: bfloat16 [1024], replicated, may hold values from -3 to 6
- head_gain: bfloat16 [512], replicated, may hold values from 0.5 to 1.5
- w_output: bfloat16 [2048, 2048], P('tensor', 'dp'), may hold values from -0.125 to 0.125
- dense_gain: bfloat16 [2048], replicated, may hold values from 0.5 to 1.5
- w_gate: bfloat16 [2048, 5632], P('dp', 'tensor'), may hold values from -0.125 to 0.125
- w_up: bfloat16 [2048, 5632], P('dp', 'tensor'), may hold values from -0.125 to 0.125
- w_down: bfloat16 [5632, 2048], P('tensor', 'dp'), may hold values from -0.078125 to 0.078125
Outputs:
- output: bfloat16 [12288, 2048], P('dp')
- grad_tokens: float32 [12288, 2048], P('dp')
- grad_mixer_gain: float32 [2048], replicated
- grad_w_query: float32 [2048, 1024], P('dp', 'tensor')
- grad_w_key: float32 [2048, 1024], P('dp', 'tensor')
- grad_w_value: float32 [2048, 2048], P('dp', 'tensor')
- grad_w_swish: float32 [2048, 2048], P('dp', 'tensor')
- grad_decay_down: float32 [2048, 16], replicated
- grad_decay_up: float32 [16, 1024], replicated
- grad_decay_bias: float32 [1024], replicated
- grad_head_gain: float32 [512], replicated
- grad_w_output: float32 [2048, 2048], P('tensor', 'dp')
- grad_dense_gain: float32 [2048], replicated
- grad_w_gate: float32 [2048, 5632], P('dp', 'tensor')
- grad_w_up: float32 [2048, 5632], P('dp', 'tensor')
- grad_w_down: float32 [5632, 2048], P('tensor', 'dp')
The draws below stay inside these ranges and needn't reach their ends.
Inputs may be any that keep to these rules, and one draw needn't show every extreme that they name: `segment_ids`: A token's segment id is the position of its document's first token. Ids never fall along the tokens, a new document starts at every multiple of 256, so no document crosses such a boundary, and the last token starts a document of its own. `w_query`: entries of order 2048^-0.5. `w_key`: entries of order 2048^-0.5.
All inputs are finite; a program needn't handle non-finite values.
Results may differ from the reference program's by a relative error of at most 0.014.
Values may be sent and summed in bfloat16 or wider, within the bound.
A program may use at most 1.1875 GiB of HBM per device.

```python
from functools import partial
import jax
import jax.numpy as jnp
from jax import lax

D = 2048
DK = 256
DV = 512
R = 16
FF = 5632
SPAN = 64
PIECE = 256
TOKENS = 12288
HK = 1024
HV = 2048


def draw_segment_ids(key, part):
    places = jnp.arange(TOKENS, dtype=jnp.int32)
    starts = (jax.random.randint(key, (TOKENS,), 0, 64) == 0) | (places % PIECE == 0) | (places == TOKENS - 1)
    marked = jnp.where(starts, places, jnp.zeros_like(places))
    return lax.cummax(marked, axis=0).astype(jnp.int32)


def query_key_pair(key):
    common = jnp.clip(jax.random.normal(jax.random.fold_in(key, 7), (D, HK), jnp.float32), -6.0, 6.0)
    own = jnp.clip(jax.random.normal(jax.random.fold_in(key, 11), (D, HK), jnp.float32), -6.0, 6.0)
    scale = D ** (-0.5)
    return (common * scale, (0.8 * common + 0.6 * own) * scale)


def draw_w_query(key, part):
    return query_key_pair(key)[0].astype(jnp.bfloat16)


def draw_w_key(key, part):
    return query_key_pair(key)[1].astype(jnp.bfloat16)


def spiked(entries, key, source, target, shards_of, factor):
    owner, partner = [(jnp.arange(entries.shape[dim]) // (entries.shape[dim] // shards_of)).reshape([-1 if axis == dim else 1 for axis in range(entries.ndim)]) for dim in (source, target)]
    chosen = jax.random.permutation(key, shards_of)[partner]
    strong = (owner == chosen) | (owner == (partner + shards_of // 2) % shards_of)
    return jnp.where(strong, factor * entries, entries)


def block_levels(rng, extent, pieces, low, largest):
    def one(axis_at, parts):
        steps = jax.random.uniform(jax.random.fold_in(jax.random.fold_in(rng, 6), axis_at), (parts,), jnp.float32, low / len(pieces), largest / len(pieces))
        return jnp.repeat(jnp.exp(steps), extent[axis_at] // parts).reshape((-1,) + (1,) * (len(extent) - axis_at - 1))

    factor_of = one(*pieces[0])
    for cut in pieces[1:]:
        factor_of = factor_of * one(*cut)
    return factor_of


def bell_draw(own_key, shape, deviation, limit, split=(), held_as=jnp.bfloat16):
    values = jax.random.normal(own_key, shape, jnp.float32) * deviation
    if len(split) > 0:
        values = block_levels(own_key, shape, split, -0.22, 0.18) * values
    return jnp.clip(values, min=-limit, max=limit).astype(held_as)


def bell_draw_with(stream_key, dims, deviation, most, cuts, heavy, held_as=jnp.bfloat16):
    drawn = deviation * jax.random.normal(stream_key, dims, jnp.float32)
    if cuts:
        drawn = drawn * block_levels(stream_key, dims, cuts, -0.22, 0.18)
    return jnp.clip(spiked(drawn, jax.random.fold_in(stream_key, 3), *heavy), -most, most).astype(held_as)


def setup_inputs(seed: int = 0) -> dict:
    streams_of = jax.random.split(jax.random.key(seed), 18)
    return {
        "tokens": bell_draw(streams_of[0], (TOKENS, D), 1.0, 6.0, ((0, 16),)),
        "segment_ids": draw_segment_ids(jax.random.fold_in(streams_of[17], 71), 0),
        "cotangent": bell_draw_with(streams_of[2], (TOKENS, D), 1.0, 6.0, ((0, 16),), (0, 1, 16, 2.0)),
        "mixer_gain": jnp.clip(1.0 + 0.1 * jax.random.normal(streams_of[3], (D,), jnp.float32), 0.5, 1.5).astype(jnp.bfloat16),
        "w_query": draw_w_query(jax.random.fold_in(streams_of[17], 71), 0),
        "w_key": draw_w_key(jax.random.fold_in(streams_of[17], 71), 0),
        "w_value": bell_draw(streams_of[6], (D, HV), D ** -0.5, 0.125, ((0, 16), (1, 2))),
        "w_swish": bell_draw(streams_of[7], (D, HV), D ** -0.5, 0.125, ((0, 16), (1, 2))),
        "decay_down": bell_draw(streams_of[8], (D, R), D ** -0.5, 0.125),
        "decay_up": bell_draw(streams_of[9], (R, HK), R ** -0.5, 1.5),
        "decay_bias": jnp.clip(jax.random.uniform(streams_of[10], (HK,), jnp.float32, -3.0, 6.0), -3.0, 6.0).astype(jnp.bfloat16),
        "head_gain": jnp.clip(1.0 + 0.1 * jax.random.normal(streams_of[11], (DV,), jnp.float32), 0.5, 1.5).astype(jnp.bfloat16),
        "w_output": bell_draw(streams_of[12], (HV, D), HV ** -0.5, 0.125, ((0, 2), (1, 16))),
        "dense_gain": jnp.clip(1.0 + 0.1 * jax.random.normal(streams_of[13], (D,), jnp.float32), 0.5, 1.5).astype(jnp.bfloat16),
        "w_gate": bell_draw(streams_of[14], (D, FF), D ** -0.5, 0.125, ((0, 16), (1, 2))),
        "w_up": bell_draw(streams_of[15], (D, FF), D ** -0.5, 0.125, ((0, 16), (1, 2))),
        "w_down": bell_draw(streams_of[16], (FF, D), FF ** -0.5, 0.078125, ((0, 2), (1, 16))),
    }


@jax.custom_vjp
def low(v):
    return lax.optimization_barrier(v.astype(jnp.bfloat16)).astype(jnp.float32)

@jax.custom_vjp
def low_back(v):
    return v

def low_keep(v):
    return (low(v), None)

def low_pass(kept, grad):
    return (grad,)

def back_keep(v):
    return (v, None)

def back_low(kept, grad):
    return (low(grad),)
low.defvjp(low_keep, low_pass)
low_back.defvjp(back_keep, back_low)
norm_eps = 1e-06
head_eps = 1e-05

def root_norm(values, eps):
    return values * lax.rsqrt(lax.optimization_barrier(jnp.mean(values * values, axis=-1, keepdims=True)) + eps)

def product_hi(left, right):
    return jnp.dot(left, right, precision=lax.Precision.HIGHEST)

def span_step(state, inputs):
    query, keyset, valueset, decay, segment, previous = inputs
    length = query.shape[0]
    running = jnp.cumsum(decay, axis=0)
    places = jnp.arange(length)
    allowed = (places[:, None] >= places[None, :]) & (segment[:, None] == segment[None, :])
    allowed = allowed[:, :, None, None]
    spread = running[:, None] - running[None, :]
    factor = jnp.where(allowed, jnp.exp(jnp.where(allowed, spread, 0.0)), 0.0)
    scores = jnp.einsum('thd,shd,tshd->tsh', query, keyset, factor, precision=lax.Precision.HIGHEST)
    inner = jnp.einsum('tsh,she->the', scores, valueset, precision=lax.Precision.HIGHEST)
    carried = (segment == previous).astype(jnp.float32)
    outer = carried[:, None, None] * jnp.einsum('thd,hde->the', query * jnp.exp(running), state, precision=lax.Precision.HIGHEST)
    final = running[-1]
    same_last = (segment == segment[-1]).astype(jnp.float32)
    moved = keyset * jnp.exp(final[None] - running) * same_last[:, None, None]
    keep_state = (segment[-1] == previous).astype(jnp.float32)
    fresh = jnp.einsum('shd,she->hde', moved, valueset, precision=lax.Precision.HIGHEST)
    new_state = keep_state * jnp.exp(final)[:, :, None] * state + fresh
    return (new_state, inner + outer)

def to_blocks(values, count):
    return values.reshape((count, SPAN) + values.shape[1:])

def gla_core(query, keyset, valueset, decay, segments):
    length, heads, width = query.shape
    count = length // SPAN
    query = query * width ** (-0.5)
    seg_blocks = segments.reshape(count, SPAN)
    previous = jnp.concatenate([jnp.full((1,), -1, jnp.int32), seg_blocks[:-1, -1].astype(jnp.int32)])
    state = jnp.zeros((heads, width, valueset.shape[-1]), jnp.float32)
    _, mixed = lax.scan(jax.checkpoint(span_step), state, (to_blocks(query, count), to_blocks(keyset, count), to_blocks(valueset, count), to_blocks(decay, count), seg_blocks, previous))
    return mixed.reshape(length, heads, valueset.shape[-1])

def mixer_core(query, keyset, valueset, decay, swish_in, gain, segments):
    length = query.shape[0]
    heads = query.shape[1] // DK
    mixed = gla_core(query.reshape(length, heads, DK), keyset.reshape(length, heads, DK), valueset.reshape(length, heads, DV), decay.reshape(length, heads, DK), segments)
    normed = root_norm(mixed, head_eps) * gain
    return (normed * jax.nn.silu(swish_in.reshape(length, heads, DV))).reshape(length, heads * DV)

def decay_gate(lowrank, up_factor, bias):
    return jax.nn.log_sigmoid(product_hi(lowrank, up_factor) + bias) / 16.0

def forward(tokens, mixer_gain, w_query, w_key, w_value, w_swish, decay_down, decay_up, decay_bias, head_gain, w_output, dense_gain, w_gate, w_up, w_down, segments):
    first = low(root_norm(tokens, norm_eps) * mixer_gain)
    query = low(low_back(product_hi(first, w_query)))
    keyset = low(low_back(product_hi(first, w_key)))
    valueset = low(low_back(product_hi(first, w_value)))
    swish_in = low_back(product_hi(first, w_swish))
    lowrank = product_hi(first, decay_down)
    decay = decay_gate(lowrank, decay_up, decay_bias)
    gated = low(mixer_core(query, keyset, valueset, decay, swish_in, head_gain, segments))
    hidden = tokens + low_back(product_hi(gated, w_output))
    second = low(root_norm(hidden, norm_eps) * dense_gain)
    gate = low_back(product_hi(second, w_gate))
    upper = low_back(product_hi(second, w_up))
    product = low(jax.nn.silu(gate) * upper)
    return hidden + low_back(product_hi(product, w_down))

def reference(tokens, segment_ids, cotangent, mixer_gain, w_query, w_key, w_value, w_swish, decay_down, decay_up, decay_bias, head_gain, w_output, dense_gain, w_gate, w_up, w_down):
    floats = tuple((array.astype(jnp.float32) for array in (tokens, mixer_gain, w_query, w_key, w_value, w_swish, decay_down, decay_up, decay_bias, head_gain, w_output, dense_gain, w_gate, w_up, w_down)))
    output, pullback = jax.vjp(partial(forward, segments=segment_ids), *floats)
    grads = pullback(cotangent.astype(jnp.float32))
    return (output.astype(jnp.bfloat16), grads[0], grads[1], grads[2], grads[3], grads[4], grads[5], grads[6], grads[7], grads[8], grads[9], grads[10], grads[11], grads[12], grads[13], grads[14])
```

```python
from functools import partial

import jax
import jax.numpy as jnp
import numpy as np
from jax import lax
from jax.experimental import pallas as pl
from jax.experimental.pallas import tpu as pltpu
from jax.sharding import PartitionSpec as P

DK = 256
DV = 512
PIECE = 256
norm_eps = 1e-06
head_eps = 1e-05
LEVELS = (1, 2, 4, 8, 16, 32, 64, 128)
f32 = jnp.float32
bf16 = jnp.bfloat16
HIGH = lax.Precision.HIGHEST


def layout(chips):
    return {16: (4, 2, 1, 2), 64: (4, 4, 2, 2)}.get(chips, (1, 1, chips // 2, 2))


def shift_pairs(sizes, axis, step):
    pairs = []
    for place in range(int(np.prod(sizes))):
        at = list(np.unravel_index(place, sizes))
        at[axis] = (at[axis] + step) % sizes[axis]
        pairs.append((place, int(np.ravel_multi_index(at, sizes))))
    return pairs


def shift(values, sizes, axis, step):
    return lax.ppermute(values, "dp", shift_pairs(sizes, axis, step))


def core_swap(values):
    return lax.ppermute(values, "tensor", [(0, 1), (1, 0)])


def in_order(index, own, other):
    return jnp.where(
        index == 0, jnp.concatenate([own, other], 0), jnp.concatenate([other, own], 0)
    )


def half(values, index, axis=0):
    size = values.shape[axis] // 2
    return lax.dynamic_slice_in_dim(values, index * size, size, axis)


def mm(left, right):
    return lax.dot_general(left, right, (((1,), (0,)), ((), ())), preferred_element_type=f32)


def mm_nt(left, right):
    return lax.dot_general(left, right, (((1,), (1,)), ((), ())), preferred_element_type=f32)


def mm_tn(left, right):
    return lax.dot_general(left, right, (((0,), (0,)), ((), ())), preferred_element_type=f32)


def reorder_kernel(places, source, target):
    count = places.shape[0]
    width = source.shape[1] // count
    for block in range(count):
        start = pl.multiple_of(places[block] * width, width)
        target[:, block * width : (block + 1) * width] = source[:, pl.ds(start, width)]


def reorder(values, places):
    rows, columns = values.shape
    count = places.shape[0]
    width = columns // count
    if width % 128 != 0:
        return jnp.concatenate(
            [lax.dynamic_slice_in_dim(values, places[i] * width, width, 1) for i in range(count)], 1
        )
    tile = 192 if rows % 192 == 0 else rows
    return pl.pallas_call(
        reorder_kernel,
        out_shape=jax.ShapeDtypeStruct(values.shape, values.dtype),
        grid_spec=pltpu.PrefetchScalarGridSpec(
            num_scalar_prefetch=1,
            grid=(rows // tile,),
            in_specs=[pl.BlockSpec((tile, columns), lambda i, p: (i, 0))],
            out_specs=pl.BlockSpec((tile, columns), lambda i, p: (i, 0)),
        ),
        cost_estimate=pl.CostEstimate(
            flops=0, bytes_accessed=2 * values.size * values.dtype.itemsize, transcendentals=0
        ),
        name="reorder",
    )(places, values)


def bit_of(shape, level):
    return (lax.broadcasted_iota(jnp.int32, shape, 0) & level) != 0


def partner(values, level, upper):
    size = values.shape[0]
    return jnp.where(
        upper, pltpu.roll(values, level, 0), pltpu.roll(values, size - level, 0)
    )


def log_decay(low, up, bias):
    pre = jnp.dot(low, up, precision=HIGH, preferred_element_type=f32) + bias
    return pre, (jnp.minimum(pre, 0.0) - jnp.log1p(jnp.exp(-jnp.abs(pre)))) * (1.0 / 16.0)


def level_exponents(decay):
    prefix, suffix, total = decay, jnp.zeros_like(decay), decay
    found = []
    for level in LEVELS:
        upper = bit_of(decay.shape, level)
        found.append(jnp.where(upper, prefix, suffix))
        if level != LEVELS[-1]:
            beside = partner(total, level, upper)
            prefix = prefix + jnp.where(upper, beside, 0.0)
            suffix = suffix + jnp.where(upper, 0.0, beside)
            total = total + beside
    return found


def pair_distance():
    rows = lax.broadcasted_iota(jnp.int32, (PIECE, PIECE), 0)
    columns = lax.broadcasted_iota(jnp.int32, (PIECE, PIECE), 1)
    return rows ^ columns, rows >= columns


def core_forward_kernel(qkv, swish, low, seg_col, seg_row, up, bias, gain, gated, scores_out, mixed_out):
    query = qkv[:, :DK].astype(f32)
    keyset = qkv[:, DK : 2 * DK].astype(f32)
    values = qkv[:, 2 * DK :]
    _, decay = log_decay(low[...], up[...], bias[...])
    apart, causal = pair_distance()
    scores = mm_nt(qkv[:, :DK], qkv[:, DK : 2 * DK])
    for level, exponent in zip(LEVELS, level_exponents(decay)):
        upper = bit_of(decay.shape, level)
        scaled = (jnp.where(upper, query, keyset) * jnp.exp(exponent)).astype(bf16)
        scores = jnp.where(apart >= level, mm_nt(scaled, scaled), scores)
    allowed = causal & (seg_col[...] == seg_row[0])
    scores = jnp.where(allowed, scores * (DK**-0.5), 0.0).astype(bf16)
    mixed = mm(scores, values)
    scores_out[...] = scores
    mixed_out[...] = mixed
    root = lax.rsqrt(jnp.mean(mixed * mixed, axis=-1, keepdims=True) + head_eps)
    opened = swish[...]
    gated[...] = (mixed * root * gain[...] * (opened * jax.nn.sigmoid(opened))).astype(bf16)


def core_backward_kernel(
    qkv, swish, low, seg_col, seg_row, up, bias, gain, scores_in, mixed_in, d_gated,
    d_qkvs, d_low, d_up, d_bias, d_gain,
):
    query = qkv[:, :DK].astype(f32)
    keyset = qkv[:, DK : 2 * DK].astype(f32)
    values = qkv[:, 2 * DK :]
    pre, decay = log_decay(low[...], up[...], bias[...])
    apart, causal = pair_distance()
    mixed = mixed_in[...]
    root = lax.rsqrt(jnp.mean(mixed * mixed, axis=-1, keepdims=True) + head_eps)
    normed = mixed * root
    opened = swish[...]
    sigma = jax.nn.sigmoid(opened)
    wanted = d_gated[...]
    d_swish = wanted * normed * gain[...] * (sigma + opened * sigma * (1.0 - sigma))
    d_scaled = wanted * (opened * sigma)
    gain_part = jnp.sum(d_scaled * normed, axis=0, keepdims=True)
    d_normed = d_scaled * gain[...]
    d_mixed = root * (d_normed - normed * jnp.mean(d_normed * normed, axis=-1, keepdims=True))
    d_mixed = d_mixed.astype(bf16)
    d_values = mm_tn(scores_in[...], d_mixed)
    allowed = causal & (seg_col[...] == seg_row[0])
    d_scores = jnp.where(allowed, mm_nt(d_mixed, values) * (DK**-0.5), 0.0)
    on_diagonal = jnp.sum(jnp.where(apart == 0, d_scores, 0.0), axis=1, keepdims=True)
    d_query = on_diagonal * keyset
    d_keyset = on_diagonal * query
    both = d_scores + d_scores.T
    exponents = level_exponents(decay)
    d_prefix = d_suffix = d_total = jnp.zeros_like(decay)
    for level, exponent in reversed(list(zip(LEVELS, exponents))):
        upper = bit_of(decay.shape, level)
        if level != LEVELS[-1]:
            d_beside = jnp.where(upper, d_prefix, d_suffix) + d_total
            d_total = d_total + partner(d_beside, level, upper)
        base = jnp.where(upper, query, keyset)
        factor = jnp.exp(exponent)
        scaled = (base * factor).astype(bf16)
        here = jnp.where((apart >= level) & (apart < 2 * level), both, 0.0).astype(bf16)
        d_base = mm(here, scaled) * factor
        d_exponent = d_base * base
        d_query = d_query + jnp.where(upper, d_base, 0.0)
        d_keyset = d_keyset + jnp.where(upper, 0.0, d_base)
        d_prefix = d_prefix + jnp.where(upper, d_exponent, 0.0)
        d_suffix = d_suffix + jnp.where(upper, 0.0, d_exponent)
    d_pre = (d_prefix + d_total) * jax.nn.sigmoid(-pre) * (1.0 / 16.0)
    d_qkvs[:, :DK] = d_query.astype(bf16)
    d_qkvs[:, DK : 2 * DK] = d_keyset.astype(bf16)
    d_qkvs[:, 2 * DK : 2 * DK + DV] = d_values.astype(bf16)
    d_qkvs[:, 2 * DK + DV :] = d_swish.astype(bf16)
    d_low[...] = lax.dot_general(
        d_pre, up[...], (((1,), (1,)), ((), ())), precision=HIGH, preferred_element_type=f32
    )

    @pl.when(pl.program_id(0) == 0)
    def _():
        d_up[...] = jnp.zeros_like(d_up)
        d_bias[...] = jnp.zeros_like(d_bias)
        d_gain[...] = jnp.zeros_like(d_gain)

    d_up[...] += lax.dot_general(
        low[...], d_pre, (((0,), (0,)), ((), ())), precision=HIGH, preferred_element_type=f32
    )
    d_bias[...] += jnp.sum(d_pre, axis=0, keepdims=True)
    d_gain[...] += gain_part


def by_piece(width):
    return pl.BlockSpec((PIECE, width), lambda i: (i, 0))


def at_once(shape):
    return pl.BlockSpec(shape, lambda i: (0,) * len(shape))


def core_specs(rank):
    return [
        by_piece(2 * DK + DV),
        by_piece(DV),
        by_piece(rank),
        by_piece(1),
        pl.BlockSpec((1, 1, PIECE), lambda i: (i, 0, 0)),
        at_once((rank, DK)),
        at_once((1, DK)),
        at_once((1, DV)),
    ]


vmem_limit = 60 * 1024 * 1024


def core_forward(qkv, swish, low, segments, up, bias, gain):
    rows, rank = low.shape
    pieces = rows // PIECE
    return pl.pallas_call(
        core_forward_kernel,
        grid=(pieces,),
        in_specs=core_specs(rank),
        out_specs=[by_piece(DV), by_piece(PIECE), by_piece(DV)],
        out_shape=[
            jax.ShapeDtypeStruct((rows, DV), bf16),
            jax.ShapeDtypeStruct((rows, PIECE), bf16),
            jax.ShapeDtypeStruct((rows, DV), f32),
        ],
        compiler_params=pltpu.CompilerParams(vmem_limit_bytes=vmem_limit),
        cost_estimate=pl.CostEstimate(
            flops=pieces * 11 * 2 * PIECE**3 * 4, bytes_accessed=rows * 9216, transcendentals=pieces * 10 * PIECE**2
        ),
        name="core_forward",
    )(qkv, swish, low, segments[:, None], segments.reshape(pieces, 1, PIECE), up, bias, gain)


def core_backward(qkv, swish, low, segments, up, bias, gain, scores, mixed, d_gated):
    rows, rank = low.shape
    pieces = rows // PIECE
    return pl.pallas_call(
        core_backward_kernel,
        grid=(pieces,),
        in_specs=core_specs(rank) + [by_piece(PIECE), by_piece(DV), by_piece(DV)],
        out_specs=[
            by_piece(2 * DK + 2 * DV),
            by_piece(rank),
            at_once((rank, DK)),
            at_once((1, DK)),
            at_once((1, DV)),
        ],
        out_shape=[
            jax.ShapeDtypeStruct((rows, 2 * DK + 2 * DV), bf16),
            jax.ShapeDtypeStruct((rows, rank), f32),
            jax.ShapeDtypeStruct((rank, DK), f32),
            jax.ShapeDtypeStruct((1, DK), f32),
            jax.ShapeDtypeStruct((1, DV), f32),
        ],
        compiler_params=pltpu.CompilerParams(vmem_limit_bytes=vmem_limit),
        cost_estimate=pl.CostEstimate(
            flops=pieces * 30 * 2 * PIECE**3 * 4, bytes_accessed=rows * 12288, transcendentals=pieces * 12 * PIECE**2
        ),
        name="core_backward",
    )(
        qkv, swish, low, segments[:, None], segments.reshape(pieces, 1, PIECE), up, bias, gain,
        scores, mixed, d_gated,
    )


def on_device(
    tokens, segment_ids, cotangent, mixer_gain, w_query, w_key, w_value, w_swish, decay_down, decay_up,
    decay_bias, head_gain, w_output, dense_gain, w_gate, w_up, w_down,
):
    sizes = layout(lax.axis_size("dp"))
    tall, deep, far, _ = sizes
    core = lax.axis_index("tensor")
    place = lax.axis_index("dp")
    near = place % 2
    far_at = (place // 2) % far
    y_at = (place // (2 * far)) % deep
    z_at = place // (2 * far * deep)
    own_rows = tokens.shape[0]
    half_rows = own_rows // 2
    width = tokens.shape[1]
    block = width // lax.axis_size("dp")

    count = tall * deep * far
    slot = jnp.arange(count, dtype=jnp.int32)
    slot_z, slot_y, slot_far = slot % tall, (slot // tall) % deep, slot // (tall * deep)
    places = (((z_at - slot_z) % tall) * deep + (y_at - slot_y) % deep) * far + (far_at - slot_far) % far
    places = places.astype(jnp.int32)
    from_z, from_y, from_far = slot // (deep * far), (slot // far) % deep, slot % far
    back = (((far_at - from_far) % far) * deep + (y_at - from_y) % deep) * tall + (z_at - from_z) % tall
    back = back.astype(jnp.int32)

    def blocks_of(values, order):
        size = values.shape[0] // count
        return jnp.concatenate(
            [lax.dynamic_slice_in_dim(values, order[i] * size, size, 0) for i in range(count)], 0
        )

    def gathered(shards):
        own = jnp.concatenate([half(shard, near, 1) for shard in shards], 1)
        other = jnp.concatenate([half(shard, 1 - near, 1) for shard in shards], 1)
        pair = in_order(near, own, shift(other, sizes, 3, 1))
        parts = [pair]
        for axis in (0, 1, 2):
            parts = parts + [
                shift(part, sizes, axis, step) for step in range(1, sizes[axis]) for part in parts
            ]
        return jnp.concatenate(parts, 0)

    w_first = gathered((w_query, w_key, w_value, w_swish))
    w_out = gathered((w_output.T,))
    w_g = gathered((w_gate,))
    w_u = gathered((w_up,))
    w_d = gathered((w_down.T,))

    def scattered(left, right):
        return finish(start(left, right))

    def start(left, right):
        slab = tall * 2 * block
        outer = deep * far
        total = None
        got = []
        for number in reversed(range(1, outer)):
            back_far, back_y = number // deep, number % deep
            sent = mm_tn(left[:, number * slab : (number + 1) * slab], right).astype(bf16)
            if back_y:
                sent = shift(sent, sizes, 1, -back_y)
            if back_far:
                sent = shift(sent, sizes, 2, -back_far)
            got.append(sent)
        total = mm_tn(left[:, :slab], right)
        for one in got:
            total = total + one.astype(f32)
        return total.astype(bf16)

    def finish(total):
        rows = 2 * block
        kept = total[:rows].astype(f32)
        for step in range(1, tall):
            kept = kept + shift(total[step * rows : (step + 1) * rows], sizes, 0, -step).astype(f32)
        received = shift(half(kept, 1 - near).astype(bf16), sizes, 3, 1).astype(f32)
        return half(kept, near), received

    def columns(parts, begin, end):
        own, received = (part[:, begin:end] for part in parts)
        return jnp.where(
            near == 0, jnp.concatenate([own, received], 1), jnp.concatenate([received, own], 1)
        )

    def whole_chip(rows):
        return in_order(core, rows, core_swap(rows))

    def from_neighbour(rows):
        return whole_chip(shift(rows, sizes, 3, 1))

    def summed_rows(partial_next, partial_own):
        handed = core_swap(half(partial_next, 1 - core))
        ahead = (half(partial_next, core).astype(f32) + handed.astype(f32)).astype(bf16)
        ahead = shift(ahead, sizes, 3, 1)
        handed_own = core_swap(half(partial_own, 1 - core))
        return half(partial_own, core).astype(f32) + handed_own.astype(f32) + ahead.astype(f32)

    seg = jnp.concatenate([segment_ids, shift(segment_ids, sizes, 3, 1)], 0)
    tok_half = half(tokens, core)
    tok_own = reorder(tokens, places)
    tok_next = reorder(from_neighbour(tok_half), places)
    cot_own = reorder(cotangent, places)
    cot_next = reorder(from_neighbour(half(cotangent, core)), places)
    tok = jnp.concatenate([tok_own, tok_next], 0)
    cot = jnp.concatenate([cot_own, cot_next], 0)
    gain_first = blocks_of(mixer_gain.astype(f32), places)
    gain_second = blocks_of(dense_gain.astype(f32), places)
    down = blocks_of(decay_down, places)
    head = 2 * core + near
    up_own = lax.dynamic_slice_in_dim(decay_up, head * DK, DK, 1).astype(f32)
    bias_own = lax.dynamic_slice_in_dim(decay_bias, head * DK, DK, 0).astype(f32)[None]
    gain_heads = head_gain.astype(f32)[None]

    def root_of(values):
        return lax.rsqrt(jnp.mean(values * values, axis=-1, keepdims=True) + norm_eps)

    tok_f = tok.astype(f32)
    first = (tok_f * root_of(tok_f) * gain_first).astype(bf16)
    low = mm(first, down)
    qkv = mm(first, w_first[:, : 2 * DK + DV]).astype(bf16)
    swish = mm(first, w_first[:, 2 * DK + DV :])
    gated, scores, mixed = core_forward(qkv, swish, low, seg, up_own, bias_own, gain_heads)

    branch = summed_rows(
        mm_nt(gated[own_rows:], w_out).astype(bf16), mm_nt(gated[:own_rows], w_out).astype(bf16)
    )
    hidden = half(tok_own, core).astype(f32) + branch
    root_hidden = root_of(hidden)
    second_half = (hidden * root_hidden * gain_second).astype(bf16)
    second_own = whole_chip(second_half)
    second_next = from_neighbour(second_half)

    def dense(second, cot_part):
        gate = mm(second, w_g)
        upper = mm(second, w_u)
        sigma = jax.nn.sigmoid(gate)
        swished = gate * sigma
        product = (swished * upper).astype(bf16)
        d_product = mm(cot_part, w_d)
        d_gate = (d_product * upper * (sigma + gate * sigma * (1.0 - sigma))).astype(bf16)
        d_up = (d_product * swished).astype(bf16)
        return product, d_gate, d_up

    product_own, d_gate_own, d_up_own = dense(second_own, cot_own)
    product_next, d_gate_next, d_up_next = dense(second_next, cot_next)
    product = jnp.concatenate([product_own, product_next], 0)
    second = jnp.concatenate([second_own, second_next], 0)
    d_gate = jnp.concatenate([d_gate_own, d_gate_next], 0)
    d_up = jnp.concatenate([d_up_own, d_up_next], 0)
    sum_d = start(cot, product)
    sum_g = start(second, d_gate)
    sum_u = start(second, d_up)

    def d_second_of(rows_gate, rows_up):
        return (mm_nt(rows_gate, w_g) + mm_nt(rows_up, w_u)).astype(bf16)

    d_second = summed_rows(d_second_of(d_gate_next, d_up_next), d_second_of(d_gate_own, d_up_own))

    dense_out = summed_rows(mm_nt(product_next, w_d).astype(bf16), mm_nt(product_own, w_d).astype(bf16))
    output = reorder(whole_chip((hidden + dense_out).astype(bf16)), back)

    def norm_pull(values, root, gain, wanted):
        scaled = wanted * gain
        return root * scaled - values * (
            root * root * root * jnp.mean(values * scaled, axis=-1, keepdims=True)
        )

    d_hidden = half(cot_own, core).astype(f32) + norm_pull(hidden, root_hidden, gain_second, d_second)
    grad_dense_gain = jnp.sum(d_second * hidden * root_hidden, axis=0)
    d_branch_half = d_hidden.astype(bf16)
    d_branch = jnp.concatenate([whole_chip(d_branch_half), from_neighbour(d_branch_half)], 0)
    sum_o = start(d_branch, gated)
    d_gated = mm(d_branch, w_out)
    d_qkvs, d_low, grad_up, grad_bias, grad_head = core_backward(
        qkv, swish, low, seg, up_own, bias_own, gain_heads, scores, mixed, d_gated
    )
    sum_first = start(first, d_qkvs)
    down_f = down.astype(f32)

    def d_first_of(begin, end):
        return (
            mm_nt(d_qkvs[begin:end], w_first) + lax.dot_general(
                d_low[begin:end], down_f, (((1,), (1,)), ((), ())), precision=HIGH, preferred_element_type=f32
            )
        ).astype(bf16)

    d_first = summed_rows(d_first_of(own_rows, 2 * own_rows), d_first_of(0, own_rows))
    tok_mine = half(tok_own, core).astype(f32)
    root_mine = root_of(tok_mine)
    grad_half = d_hidden + norm_pull(tok_mine, root_mine, gain_first, d_first)
    grad_mixer_gain = jnp.sum(d_first * tok_mine * root_mine, axis=0)
    grad_tokens = reorder(whole_chip(grad_half), back)
    grad_down = lax.dot_general(
        first.astype(f32), d_low, (((0,), (0,)), ((), ())), precision=HIGH, preferred_element_type=f32
    )
    small = (
        blocks_of(grad_mixer_gain, back),
        blocks_of(grad_dense_gain, back),
        grad_head[0],
        blocks_of(grad_down, back),
        lax.dynamic_update_slice_in_dim(jnp.zeros(decay_up.shape, f32), grad_up, head * DK, 1),
        lax.dynamic_update_slice_in_dim(jnp.zeros(decay_bias.shape, f32), grad_bias[0], head * DK, 0),
    )
    small = lax.psum(small, ("dp", "tensor"))

    out_d, out_g, out_u = finish(sum_d), finish(sum_g), finish(sum_u)
    out_o, out_first = finish(sum_o), finish(sum_first)

    def all_of(parts):
        return columns(parts, 0, parts[0].shape[1])

    return (
        output,
        grad_tokens,
        small[0],
        columns(out_first, 0, DK),
        columns(out_first, DK, 2 * DK),
        columns(out_first, 2 * DK, 2 * DK + DV),
        columns(out_first, 2 * DK + DV, 2 * DK + 2 * DV),
        small[3],
        small[4],
        small[5],
        small[2],
        all_of(out_o).T,
        small[1],
        all_of(out_g),
        all_of(out_u),
        all_of(out_d).T,
    )


def solution(mesh):
    rows, large, turned, whole = P("dp", None), P("dp", "tensor"), P("tensor", "dp"), P()
    in_specs = (
        rows, P("dp"), rows, whole, large, large, large, large, whole, whole, whole, whole, turned,
        whole, large, large, turned,
    )
    out_specs = (
        rows, rows, whole, large, large, large, large, whole, whole, whole, whole, turned, whole,
        large, large, turned,
    )
    return jax.shard_map(on_device, mesh=mesh, in_specs=in_specs, out_specs=out_specs, check_vma=False)
```

```python
from functools import partial

import jax
import jax.numpy as jnp
import numpy as np
from jax import lax
from jax.experimental import pallas as pl
from jax.experimental.pallas import tpu as pltpu
from jax.sharding import PartitionSpec as P

DK = 256
DV = 512
PIECE = 256
norm_eps = 1e-06
head_eps = 1e-05
LEVELS = (1, 2, 4, 8, 16, 32, 64, 128)
f32 = jnp.float32
bf16 = jnp.bfloat16
HIGH = lax.Precision.HIGHEST


def layout(chips):
    return {16: (4, 2, 1, 2), 64: (4, 4, 2, 2)}.get(chips, (1, 1, chips // 2, 2))


def split_place(place, sizes):
    _, deep, far, _ = sizes
    near = lax.rem(place, np.int32(2))
    far_at = lax.rem(lax.div(place, np.int32(2)), np.int32(far))
    y_at = lax.rem(lax.div(place, np.int32(2 * far)), np.int32(deep))
    return lax.div(place, np.int32(2 * far * deep)), y_at, far_at, near


def shift_pairs(sizes, axis, step):
    pairs = []
    for place in range(int(np.prod(sizes))):
        at = list(np.unravel_index(place, sizes))
        at[axis] = (at[axis] + step) % sizes[axis]
        pairs.append((place, int(np.ravel_multi_index(at, sizes))))
    return pairs


def exchange_pairs(sizes, axis, reach):
    pairs = []
    for place in range(int(np.prod(sizes))):
        at = list(np.unravel_index(place, sizes))
        at[axis] ^= reach
        pairs.append((place, int(np.ravel_multi_index(at, sizes))))
    return pairs


def shift(values, sizes, axis, step):
    return lax.ppermute(values, "dp", shift_pairs(sizes, axis, step))


def hop_pairs(sizes, axis, step, distance):
    pairs = []
    for place in range(int(np.prod(sizes))):
        at = list(np.unravel_index(place, sizes))
        behind = at[axis] if step > 0 else sizes[axis] - 1 - at[axis]
        at[axis] += step
        if behind >= distance - 1 and 0 <= at[axis] < sizes[axis]:
            pairs.append((place, int(np.ravel_multi_index(at, sizes))))
    return pairs


def reach_pairs(sizes, axis, step, reach):
    pairs = []
    for place in range(int(np.prod(sizes))):
        at = list(np.unravel_index(place, sizes))
        if 0 <= at[axis] + step * reach < sizes[axis]:
            at[axis] += step
            pairs.append((place, int(np.ravel_multi_index(at, sizes))))
    return pairs


class Link:
    def __init__(self, window):
        self.window, self.landed = window, []

    def send(self, move, values, *others):
        earlier = self.landed[-self.window :][:1] if len(self.landed) >= self.window else []
        ties = tuple(others) + tuple(earlier)
        landed = move(after(values, *ties) if ties else values)
        self.landed.append(landed)
        return landed


def after(values, *others):
    return lax.optimization_barrier((values,) + tuple(jax.tree.leaves(others)))[0]


def core_swap(values):
    return lax.ppermute(values, "tensor", [(0, 1), (1, 0)])


def in_order(index, own, other):
    return jnp.where(
        index == 0, jnp.concatenate([own, other], 0), jnp.concatenate([other, own], 0)
    )


def half(values, index, axis=0):
    size = values.shape[axis] // 2
    return lax.dynamic_slice_in_dim(values, index * size, size, axis)


def mm(left, right):
    return lax.dot_general(left, right, (((1,), (0,)), ((), ())), preferred_element_type=f32)


def mm_nt(left, right):
    return lax.dot_general(left, right, (((1,), (1,)), ((), ())), preferred_element_type=f32)


def mm_tn(left, right):
    return lax.dot_general(left, right, (((0,), (0,)), ((), ())), preferred_element_type=f32)


def reorder_kernel(places, source, target):
    count = places.shape[0]
    width = source.shape[1] // count
    for block in range(count):
        start = pl.multiple_of(places[block] * width, width)
        target[:, block * width : (block + 1) * width] = source[:, pl.ds(start, width)]


def reorder(values, places):
    rows, columns = values.shape
    count = places.shape[0]
    width = columns // count
    if width % 128 != 0:
        return jnp.concatenate(
            [lax.dynamic_slice_in_dim(values, places[i] * width, width, 1) for i in range(count)], 1
        )
    tile = 192 if rows % 192 == 0 else rows
    return pl.pallas_call(
        reorder_kernel,
        out_shape=jax.ShapeDtypeStruct(values.shape, values.dtype),
        grid_spec=pltpu.PrefetchScalarGridSpec(
            num_scalar_prefetch=1,
            grid=(rows // tile,),
            in_specs=[pl.BlockSpec((tile, columns), lambda i, p: (i, 0))],
            out_specs=pl.BlockSpec((tile, columns), lambda i, p: (i, 0)),
        ),
        cost_estimate=pl.CostEstimate(
            flops=0, bytes_accessed=2 * values.size * values.dtype.itemsize, transcendentals=0
        ),
        name="reorder",
    )(places, values)


def bit_of(shape, level):
    return (lax.broadcasted_iota(jnp.int32, shape, 0) & level) != 0


def partner(values, level, upper):
    size = values.shape[0]
    return jnp.where(
        upper, pltpu.roll(values, level, 0), pltpu.roll(values, size - level, 0)
    )


def log_decay(low, up, bias):
    pre = jnp.dot(low, up, precision=HIGH, preferred_element_type=f32) + bias
    return pre, (jnp.minimum(pre, 0.0) - jnp.log1p(jnp.exp(-jnp.abs(pre)))) * (1.0 / 16.0)


def level_exponents(decay):
    prefix, suffix, total = decay, jnp.zeros_like(decay), decay
    found = []
    for level in LEVELS:
        upper = bit_of(decay.shape, level)
        found.append(jnp.where(upper, prefix, suffix))
        if level != LEVELS[-1]:
            beside = partner(total, level, upper)
            prefix = prefix + jnp.where(upper, beside, 0.0)
            suffix = suffix + jnp.where(upper, 0.0, beside)
            total = total + beside
    return found


def pair_distance():
    rows = lax.broadcasted_iota(jnp.int32, (PIECE, PIECE), 0)
    columns = lax.broadcasted_iota(jnp.int32, (PIECE, PIECE), 1)
    return rows ^ columns, rows >= columns


def fixed(shape):
    return pl.BlockSpec(shape, lambda i: (0,) * len(shape), pipeline_mode=pl.Buffered(1))


def by_rows(tile, width):
    return pl.BlockSpec((tile, width), lambda i: (i, 0))


def shape_of(rows, width, kind):
    return jax.ShapeDtypeStruct((rows, width), kind)


vmem_limit = 60 * 1024 * 1024


def call(kernel, name, grid, in_specs, out_specs, out_shape):
    return pl.pallas_call(
        kernel,
        grid=grid,
        in_specs=in_specs,
        out_specs=out_specs,
        out_shape=out_shape,
        compiler_params=pltpu.CompilerParams(vmem_limit_bytes=vmem_limit),
        cost_estimate=pl.CostEstimate(flops=1, bytes_accessed=1, transcendentals=0),
        name=name,
    )


def piece_attention(query_low, keyset_low, decay):
    query, keyset = query_low.astype(f32), keyset_low.astype(f32)
    apart, causal = pair_distance()
    scores = mm_nt(query_low, keyset_low)
    for level, exponent in zip(LEVELS, level_exponents(decay)):
        upper = bit_of(decay.shape, level)
        scaled = (jnp.where(upper, query, keyset) * jnp.exp(exponent)).astype(bf16)
        scores = jnp.where(apart >= level, mm_nt(scaled, scaled), scores)
    return scores, causal


def mixer_forward_kernel(
    tok, w_first, down, gain_first, seg_col, seg_row, up, bias, gain,
    first_out, low_out, qkv_out, swish_out, scores_out, mixed_out, gated_out,
):
    rows = tok[...].astype(f32)
    root_rows = lax.rsqrt(jnp.mean(rows * rows, axis=-1, keepdims=True) + norm_eps)
    first = (rows * root_rows * gain_first[...]).astype(bf16)
    first_out[...] = first
    low = mm(first, down[...])
    low_out[...] = low
    qkv = mm(first, w_first[:, : 2 * DK + DV]).astype(bf16)
    qkv_out[...] = qkv
    opened = mm(first, w_first[:, 2 * DK + DV :])
    swish_out[...] = opened
    _, decay = log_decay(low, up[...], bias[...])
    scores, causal = piece_attention(qkv[:, :DK], qkv[:, DK : 2 * DK], decay)
    allowed = causal & (seg_col[...] == seg_row[0])
    scores = jnp.where(allowed, scores * (DK**-0.5), 0.0).astype(bf16)
    mixed = mm(scores, qkv[:, 2 * DK :])
    scores_out[...] = scores
    mixed_out[...] = mixed
    root = lax.rsqrt(jnp.mean(mixed * mixed, axis=-1, keepdims=True) + head_eps)
    gated_out[...] = (mixed * root * gain[...] * (opened * jax.nn.sigmoid(opened))).astype(bf16)


def mixer_forward(tok, w_first, down, gain_first, segments, up, bias, gain):
    rows, width = tok.shape
    rank = down.shape[1]
    pieces = rows // PIECE
    return call(
        mixer_forward_kernel, "mixer_forward", (pieces,),
        [
            by_rows(PIECE, width), fixed(w_first.shape), fixed(down.shape), fixed((1, width)),
            by_rows(PIECE, 1), pl.BlockSpec((1, 1, PIECE), lambda i: (i, 0, 0)),
            fixed(up.shape), fixed(bias.shape), fixed(gain.shape),
        ],
        [
            by_rows(PIECE, width), by_rows(PIECE, rank), by_rows(PIECE, 2 * DK + DV), by_rows(PIECE, DV),
            by_rows(PIECE, PIECE), by_rows(PIECE, DV), by_rows(PIECE, DV),
        ],
        [
            shape_of(rows, width, bf16), shape_of(rows, rank, f32), shape_of(rows, 2 * DK + DV, bf16),
            shape_of(rows, DV, f32), shape_of(rows, PIECE, bf16), shape_of(rows, DV, f32), shape_of(rows, DV, bf16),
        ],
    )(tok, w_first, down, gain_first, segments[:, None], segments.reshape(pieces, 1, PIECE), up, bias, gain)


def product_nt_kernel(left, right, out):
    out[...] = mm_nt(left[...], right[...]).astype(bf16)


def product_nt(left, right):
    rows, width = left.shape[0], right.shape[0]
    return call(
        product_nt_kernel, "product_nt", (rows // 256,),
        [by_rows(256, left.shape[1]), fixed(right.shape)], by_rows(256, width), shape_of(rows, width, bf16),
    )(left, right)


def mixer_backward_kernel(
    d_branch, w_out, w_first, down, qkv, swish, low, seg_col, seg_row, up, bias, gain, scores_in, mixed_in,
    d_qkvs, d_low_out, d_first, d_up, d_bias, d_gain,
):
    query = qkv[:, :DK].astype(f32)
    keyset = qkv[:, DK : 2 * DK].astype(f32)
    values = qkv[:, 2 * DK :]
    pre, decay = log_decay(low[...], up[...], bias[...])
    apart, causal = pair_distance()
    mixed = mixed_in[...]
    root = lax.rsqrt(jnp.mean(mixed * mixed, axis=-1, keepdims=True) + head_eps)
    normed = mixed * root
    opened = swish[...]
    sigma = jax.nn.sigmoid(opened)
    wanted = mm(d_branch[...], w_out[...])
    d_swish = (wanted * normed * gain[...] * (sigma + opened * sigma * (1.0 - sigma))).astype(bf16)
    d_scaled = wanted * (opened * sigma)
    gain_part = jnp.sum(d_scaled * normed, axis=0, keepdims=True)
    d_normed = d_scaled * gain[...]
    d_mixed = root * (d_normed - normed * jnp.mean(d_normed * normed, axis=-1, keepdims=True))
    d_mixed = d_mixed.astype(bf16)
    d_values = mm_tn(scores_in[...], d_mixed).astype(bf16)
    allowed = causal & (seg_col[...] == seg_row[0])
    d_scores = jnp.where(allowed, mm_nt(d_mixed, values) * (DK**-0.5), 0.0)
    on_diagonal = jnp.sum(jnp.where(apart == 0, d_scores, 0.0), axis=1, keepdims=True)
    d_query = on_diagonal * keyset
    d_keyset = on_diagonal * query
    both = d_scores + d_scores.T
    exponents = level_exponents(decay)
    d_prefix = d_suffix = d_total = jnp.zeros_like(decay)
    for level, exponent in reversed(list(zip(LEVELS, exponents))):
        upper = bit_of(decay.shape, level)
        if level != LEVELS[-1]:
            d_beside = jnp.where(upper, d_prefix, d_suffix) + d_total
            d_total = d_total + partner(d_beside, level, upper)
        base = jnp.where(upper, query, keyset)
        factor = jnp.exp(exponent)
        scaled = (base * factor).astype(bf16)
        here = jnp.where((apart >= level) & (apart < 2 * level), both, 0.0).astype(bf16)
        d_base = mm(here, scaled) * factor
        d_exponent = d_base * base
        d_query = d_query + jnp.where(upper, d_base, 0.0)
        d_keyset = d_keyset + jnp.where(upper, 0.0, d_base)
        d_prefix = d_prefix + jnp.where(upper, d_exponent, 0.0)
        d_suffix = d_suffix + jnp.where(upper, 0.0, d_exponent)
    d_pre = (d_prefix + d_total) * jax.nn.sigmoid(-pre) * (1.0 / 16.0)
    d_query, d_keyset = d_query.astype(bf16), d_keyset.astype(bf16)
    d_qkvs[:, :DK] = d_query
    d_qkvs[:, DK : 2 * DK] = d_keyset
    d_qkvs[:, 2 * DK : 2 * DK + DV] = d_values
    d_qkvs[:, 2 * DK + DV :] = d_swish
    d_low = lax.dot_general(
        d_pre, up[...], (((1,), (1,)), ((), ())), precision=HIGH, preferred_element_type=f32
    )
    d_low_out[...] = d_low
    d_first[...] = (
        mm_nt(d_query, w_first[:, :DK])
        + mm_nt(d_keyset, w_first[:, DK : 2 * DK])
        + mm_nt(d_values, w_first[:, 2 * DK : 2 * DK + DV])
        + mm_nt(d_swish, w_first[:, 2 * DK + DV :])
        + lax.dot_general(
            d_low, down[...].astype(f32), (((1,), (1,)), ((), ())), precision=HIGH, preferred_element_type=f32
        )
    ).astype(bf16)

    @pl.when(pl.program_id(0) == 0)
    def _():
        d_up[...] = jnp.zeros_like(d_up)
        d_bias[...] = jnp.zeros_like(d_bias)
        d_gain[...] = jnp.zeros_like(d_gain)

    d_up[...] += lax.dot_general(
        low[...], d_pre, (((0,), (0,)), ((), ())), precision=HIGH, preferred_element_type=f32
    )
    d_bias[...] += jnp.sum(d_pre, axis=0, keepdims=True)
    d_gain[...] += gain_part


def at_once(shape):
    return pl.BlockSpec(shape, lambda i: (0,) * len(shape))


def mixer_backward(d_branch, w_out, w_first, down, qkv, swish, low, segments, up, bias, gain, scores, mixed):
    rows, width = d_branch.shape
    rank = low.shape[1]
    pieces = rows // PIECE
    return call(
        mixer_backward_kernel, "mixer_backward", (pieces,),
        [
            by_rows(PIECE, width), fixed(w_out.shape), fixed(w_first.shape), fixed(down.shape),
            by_rows(PIECE, 2 * DK + DV), by_rows(PIECE, DV), by_rows(PIECE, rank), by_rows(PIECE, 1),
            pl.BlockSpec((1, 1, PIECE), lambda i: (i, 0, 0)), fixed(up.shape), fixed(bias.shape), fixed(gain.shape),
            by_rows(PIECE, PIECE), by_rows(PIECE, DV),
        ],
        [
            by_rows(PIECE, 2 * DK + 2 * DV), by_rows(PIECE, rank), by_rows(PIECE, width),
            at_once((rank, DK)), at_once((1, DK)), at_once((1, DV)),
        ],
        [
            shape_of(rows, 2 * DK + 2 * DV, bf16), shape_of(rows, rank, f32), shape_of(rows, width, bf16),
            shape_of(rank, DK, f32), shape_of(1, DK, f32), shape_of(1, DV, f32),
        ],
    )(
        d_branch, w_out, w_first, down, qkv, swish, low, segments[:, None], segments.reshape(pieces, 1, PIECE),
        up, bias, gain, scores, mixed,
    )


def dense_forward_kernel(second, w_g, w_u, gate_out, upper_out, product_out):
    gate = mm(second[...], w_g[...])
    gate_out[...] = gate
    upper = mm(second[...], w_u[...])
    upper_out[...] = upper
    product_out[...] = (gate * jax.nn.sigmoid(gate) * upper).astype(bf16)


def dense_forward(second, w_g, w_u):
    rows, width = second.shape
    units = w_g.shape[1]
    return call(
        dense_forward_kernel, "dense_forward", (rows // 256,),
        [by_rows(256, width), fixed(w_g.shape), fixed(w_u.shape)], [by_rows(256, units)] * 3,
        [shape_of(rows, units, f32), shape_of(rows, units, f32), shape_of(rows, units, bf16)],
    )(second, w_g, w_u)


def dense_backward_kernel(cot, w_d, w_g, w_u, gate_in, upper_in, d_gate_out, d_up_out, d_second):
    gate = gate_in[...]
    sigma = jax.nn.sigmoid(gate)
    d_product = mm(cot[...], w_d[...])
    d_gate = (d_product * upper_in[...] * (sigma + gate * sigma * (1.0 - sigma))).astype(bf16)
    d_up = (d_product * (gate * sigma)).astype(bf16)
    d_gate_out[...] = d_gate
    d_up_out[...] = d_up
    d_second[...] = (mm_nt(d_gate, w_g[...]) + mm_nt(d_up, w_u[...])).astype(bf16)


def dense_backward(cot, w_d, w_g, w_u, gate, upper):
    rows, width = cot.shape
    units = w_g.shape[1]
    return call(
        dense_backward_kernel, "dense_backward", (rows // 256,),
        [by_rows(256, width), fixed(w_d.shape), fixed(w_g.shape), fixed(w_u.shape)] + [by_rows(256, units)] * 2,
        [by_rows(256, units), by_rows(256, units), by_rows(256, width)],
        [shape_of(rows, units, bf16), shape_of(rows, units, bf16), shape_of(rows, width, bf16)],
    )(cot, w_d, w_g, w_u, gate, upper)


def slab_kernel(others, left_own, left_next, right_own, right_next, *rest):
    total = mm_tn(left_own[...], right_own[...]) + mm_tn(left_next[...], right_next[...])
    for other in rest[:others]:
        total = total + other[...].astype(f32)
    rest[others][...] = total.astype(bf16)


def slab_gradient(left, right, begin, rows, received):
    count, width = right[0].shape
    tile = 256 if rows % 256 == 0 else 128
    at = begin // tile
    column_block = pl.BlockSpec((count, tile), lambda i: (0, at + i))
    return call(
        partial(slab_kernel, len(received)), "slab_gradient", (rows // tile,),
        [column_block] * 2 + [fixed((count, width))] * 2 + [by_rows(tile, width)] * len(received),
        by_rows(tile, width), shape_of(rows, width, bf16),
    )(*left, *right, *received)


def opening_kernel(sizes, counts, *refs):
    groups, full, row_count = counts
    tall, deep, far, _ = sizes
    refs = list(refs)
    owns, others = refs[:groups], refs[groups : 2 * groups]
    rows_in = refs[2 * groups : 2 * groups + row_count]
    seg_in = refs[2 * groups + row_count]
    outs = refs[2 * groups + row_count + 1 :]
    weights, rows_out, seg_out = outs[:groups], outs[groups : groups + row_count], outs[groups + row_count]
    local_sem, x_sem, z_sem, y_sem, row_sem, core_sem, seg_sem = outs[groups + row_count + 1 :]

    place, core = lax.axis_index("dp"), lax.axis_index("tensor")
    near = place % 2
    far_at = (place // 2) % far
    y_at = (place // (2 * far)) % deep
    z_at = place // (2 * far * deep)

    def device(z, y, far_x, near_x, which):
        return (((z * deep + y) * far + far_x) * 2 + near_x, which)

    beside = device(z_at, y_at, far_at, 1 - near, core)
    other_core = device(z_at, y_at, far_at, near, 1 - core)
    above = device(z_at + 1, y_at, far_at, near, core)
    below = device(z_at - 1, y_at, far_at, near, core)
    has_above, has_below = z_at + 1 < tall, z_at >= 1
    shifts = [(fr, yr) for fr in range(far) for yr in range(deep) if fr or yr]
    peers = [device(z_at, (y_at + yr) % deep, (far_at + fr) % far, near, core) for fr, yr in shifts]

    barrier = pltpu.get_barrier_semaphore()

    def greet(who):
        pl.semaphore_signal(barrier, inc=1, device_id=who, device_id_type=pl.DeviceIdType.MESH)

    greet(beside)
    greet(other_core)
    for peer in peers:
        greet(peer)
    pl.when(has_above)(lambda: greet(above))
    pl.when(has_below)(lambda: greet(below))
    along = has_above.astype(jnp.int32) + has_below.astype(jnp.int32)
    pl.semaphore_wait(barrier, 2 + len(peers) + along)

    def remote(source, target, sems, index, who):
        return pltpu.make_async_remote_copy(
            src_ref=source, dst_ref=target, send_sem=sems.at[(0,) + index], recv_sem=sems.at[(1,) + index],
            device_id=who, device_id_type=pl.DeviceIdType.MESH,
        )

    block = owns[0].shape[0]
    size = 2 * block

    def slab(group, number, back):
        return weights[group].at[pl.ds((number * tall + back) * size, size)]

    def own_part(group):
        return weights[group].at[pl.ds(pl.multiple_of(near * block, block), block)]

    def local(group):
        return pltpu.make_async_copy(owns[group], own_part(group), local_sem.at[group])

    def crossing(group):
        return remote(others[group], own_part(group), x_sem, (group,), beside)

    def rising(group, hop):
        return remote(slab(group, 0, hop - 1), slab(group, 0, hop), z_sem, (group, 0, hop - 1), above)

    def falling(group, hop):
        return remote(
            slab(group, 0, (tall - hop + 1) % tall), slab(group, 0, tall - hop), z_sem, (group, 1, hop - 1), below
        )

    def sideways(group, number, back):
        return remote(
            slab(group, 0, back), slab(group, number + 1, back), y_sem, (group, number, back), peers[number]
        )

    half_rows = rows_in[0].shape[0]

    def mine(array):
        return rows_out[array].at[pl.ds(pl.multiple_of(core * half_rows, half_rows), half_rows)]

    def rows_crossing(array):
        return remote(rows_in[array], mine(array), row_sem, (array,), beside)

    def rows_sharing(array):
        return remote(mine(array), mine(array), core_sem, (array,), other_core)

    def seg_crossing():
        return remote(seg_in, seg_out, seg_sem, (0,), beside)

    def spread(group, back):
        for number in range(len(peers)):
            sideways(group, number, back).start()

    def step_z(group, hop):
        @pl.when(z_at >= hop)
        def _():
            rising(group, hop).wait_recv()

        if hop + 1 < tall:
            @pl.when((z_at >= hop) & has_above)
            def _():
                rising(group, hop + 1).start()

        @pl.when(z_at + hop < tall)
        def _():
            falling(group, hop).wait_recv()

        if hop + 1 < tall:
            @pl.when((z_at + hop < tall) & has_below)
            def _():
                falling(group, hop + 1).start()

        @pl.when(z_at >= hop)
        def _():
            spread(group, hop)

        @pl.when(z_at + hop < tall)
        def _():
            spread(group, tall - hop)

    def arrive(group):
        local(group).wait()
        crossing(group).wait_recv()

    def first_hop(group):
        pl.when(has_above)(lambda: rising(group, 1).start())
        pl.when(has_below)(lambda: falling(group, 1).start())

    crossing(0).start()
    for group in range(groups):
        local(group).start()
    arrive(0)
    first_hop(0)
    spread(0, 0)
    for group in range(1, groups):
        crossing(group).start()
    seg_crossing().start()
    for array in range(row_count):
        rows_crossing(array).start()
    for group in range(1, full):
        arrive(group)
        spread(group, 0)
    for hop in range(1, tall):
        step_z(0, hop)
        if hop == tall - 2 or tall == 2:
            for group in range(1, full):
                first_hop(group)
    for group in range(1, full):
        for hop in range(1, tall):
            step_z(group, hop)
    for array in range(row_count):
        rows_crossing(array).wait_recv()
        rows_sharing(array).start()
    for group in range(full, groups):
        arrive(group)
    for group in range(full):
        for number in range(len(peers)):
            for back in range(tall):
                sideways(group, number, back).wait()
        for hop in range(1, tall):
            pl.when((z_at >= hop - 1) & has_above)(lambda hop=hop: rising(group, hop).wait_send())
            pl.when((z_at + hop - 1 < tall) & has_below)(lambda hop=hop: falling(group, hop).wait_send())
    for group in range(groups):
        crossing(group).wait_send()
    for array in range(row_count):
        rows_crossing(array).wait_send()
        rows_sharing(array).wait()
    seg_crossing().wait()


def opening(sizes, full, owns, others, rows, segments):
    tall, deep, far, _ = sizes
    groups, row_count = len(owns), len(rows)
    block = owns[0].shape[0]
    blocks = tall * deep * far
    anywhere = pl.BlockSpec(memory_space=pl.ANY)
    seg = segments.reshape(-1, 128)
    outs = [
        shape_of(2 * block * (blocks if group < full else 1), own.shape[1], bf16) for group, own in enumerate(owns)
    ]
    outs += [shape_of(2 * one.shape[0], one.shape[1], bf16) for one in rows] + [shape_of(*seg.shape, jnp.int32)]
    dma = pltpu.SemaphoreType.DMA
    peers = deep * far - 1
    results = pl.pallas_call(
        partial(opening_kernel, sizes, (groups, full, row_count)),
        in_specs=[anywhere] * (2 * groups + row_count + 1),
        out_specs=[anywhere] * len(outs),
        out_shape=outs,
        scratch_shapes=[
            dma((groups,)), dma((2, groups)), dma((2, full, 2, tall - 1)), dma((2, full, peers, tall)),
            dma((2, row_count)), dma((2, row_count)), dma((2, 1)),
        ],
        compiler_params=pltpu.CompilerParams(
            collective_id=0, has_side_effects=True, vmem_limit_bytes=vmem_limit
        ),
        cost_estimate=pl.CostEstimate(flops=1, bytes_accessed=1, transcendentals=0),
        name="opening",
    )(*owns, *others, *rows, seg)
    return results[:groups], results[groups : groups + row_count], results[-1].reshape(-1)


def on_device(
    tokens, segment_ids, cotangent, mixer_gain, w_query, w_key, w_value, w_swish, decay_down, decay_up,
    decay_bias, head_gain, w_output, dense_gain, w_gate, w_up, w_down,
):
    sizes = layout(lax.axis_size("dp"))
    tall, deep, far, _ = sizes
    core = lax.axis_index("tensor")
    place = lax.axis_index("dp")
    z_at, y_at, far_at, near = split_place(place, sizes)
    own_rows = tokens.shape[0]
    half_rows = own_rows // 2
    width = tokens.shape[1]
    block = width // lax.axis_size("dp")

    count = tall * deep * far
    slot = np.arange(count, dtype=np.int32)
    slot_z, slot_y, slot_far = slot % tall, (slot // tall) % deep, slot // (tall * deep)
    from_z, from_y, from_far = slot // (deep * far), (slot // far) % deep, slot % far

    def counted(at, backwards, size):
        return lax.rem(at + (size - backwards), np.int32(size))

    places = (counted(z_at, slot_z, tall) * deep + counted(y_at, slot_y, deep)) * far + counted(far_at, slot_far, far)
    back = (counted(far_at, from_far, far) * deep + counted(y_at, from_y, deep)) * tall + counted(z_at, from_z, tall)

    def blocks_of(values, order):
        chosen = (order[:, None] == slot[None, :]).astype(f32)
        flat = values.astype(f32).reshape(count, -1)
        return jnp.dot(chosen, flat, precision=HIGH).reshape(values.shape)

    def halves(*shards):
        own = jnp.concatenate([half(shard, near, 1) for shard in shards], 1)
        other = jnp.concatenate([half(shard, 1 - near, 1) for shard in shards], 1)
        return own, other

    x_link, y_link, z_link = Link(1), Link(2), Link(4)

    def cross(values, *others):
        return x_link.send(lambda v: shift(v, sizes, 3, 1), values, *others)

    def along_z(pair):
        up = down = pair
        ups, downs = [], []
        for hop in range(1, tall):
            up = z_link.send(lambda v: lax.ppermute(v, "dp", hop_pairs(sizes, 0, 1, hop)), up)
            down = z_link.send(lambda v: lax.ppermute(v, "dp", hop_pairs(sizes, 0, -1, hop)), down)
            ups.append(up)
            downs.append(down)
        return [jnp.where(z_at >= back, ups[back - 1], downs[tall - back - 1]) for back in range(1, tall)]

    def along_y(part, *others):
        found = [part]
        for axis in (1, 2):
            found = found + [
                y_link.send(lambda v: shift(v, sizes, axis, step), one, *others)
                for step in range(1, sizes[axis]) for one in found
            ]
        return found[1:]

    def stacked(columns):
        return jnp.concatenate([column[i] for i in range(deep * far) for column in columns], 0)

    z_order = sorted(range(1, tall), key=lambda back: max(back, tall - back))

    def z_then_y(pair, along, rest, ties):
        columns = [[pair] + rest] + [None] * (tall - 1)
        for back, tie in zip(z_order, ties):
            columns[back] = [along[back - 1]] + along_y(along[back - 1], *tie)
        return stacked(columns)

    def y_then_z(pair, rest):
        slab = jnp.concatenate([pair] + rest, 0)
        size = pair.shape[0]
        slabs = [slab] + along_z(slab)
        return stacked([[one[i * size : (i + 1) * size] for i in range(deep * far)] for one in slabs])

    halved = [
        halves(w_query, w_key, w_value, w_swish), halves(w_output.T), halves(w_gate), halves(w_up), halves(w_down.T)
    ]
    (w_first, w_out, pair_g, pair_u, pair_d), (tok_next, cot_next), seg_next = opening(
        sizes, 2, [own for own, _ in halved], [other for _, other in halved],
        [half(tokens, core), half(cotangent, core)], segment_ids,
    )
    along_g = along_z(pair_g)
    rest_g = along_y(pair_g)
    rest_u, rest_d = along_y(pair_u), along_y(pair_d)
    along_u = along_z(pair_u)

    def slabs(left, right):
        slab = tall * 2 * block
        outer = deep * far
        made = [slab_gradient(left, right, number * slab, slab, ()) for number in reversed(range(1, outer))]
        return made if outer == 2 else (tuple(made),)

    def sent_y(made):
        received = []
        outer = deep * far
        for number, sent in zip(reversed(range(1, outer)), (made,) if outer == 2 else made):
            back_far, back_y = number // deep, number % deep
            if back_y:
                sent = y_link.send(lambda v: shift(v, sizes, 1, -back_y), sent)
            if back_far:
                sent = shift(sent, sizes, 2, -back_far)
            received.append(sent)
        return received

    def own_slab(left, right, received):
        return slab_gradient(left, right, 0, tall * 2 * block, received)

    def finish(total):
        rows = 2 * block
        parts = [total[step * rows : (step + 1) * rows] for step in range(tall)]
        up = down = None
        for hop in range(1, tall):
            reach = tall - hop
            rising, falling = parts[tall - reach], parts[reach]
            if up is not None:
                rising = (rising.astype(f32) + up.astype(f32)).astype(bf16)
                falling = (falling.astype(f32) + down.astype(f32)).astype(bf16)
            up = z_link.send(lambda v: lax.ppermute(v, "dp", reach_pairs(sizes, 0, 1, reach)), rising)
            down = z_link.send(lambda v: lax.ppermute(v, "dp", reach_pairs(sizes, 0, -1, reach)), falling)
        kept = parts[0].astype(f32) + up.astype(f32) + down.astype(f32)
        received = shift(half(kept, 1 - near).astype(bf16), sizes, 3, 1).astype(f32)
        return half(kept, near), received

    def columns(parts, begin, end):
        own, received = (part[:, begin:end] for part in parts)
        return jnp.where(
            near == 0, jnp.concatenate([own, received], 1), jnp.concatenate([received, own], 1)
        )

    def whole_chip(rows):
        return in_order(core, rows, core_swap(rows))

    def from_neighbour(rows):
        return whole_chip(cross(rows))

    def summed_ahead(partial_next):
        handed = core_swap(half(partial_next, 1 - core))
        ahead = (half(partial_next, core).astype(f32) + handed.astype(f32)).astype(bf16)
        return cross(ahead)

    def summed_here(partial_own, ahead):
        handed = core_swap(half(partial_own, 1 - core))
        return half(partial_own, core).astype(f32) + handed.astype(f32) + ahead.astype(f32)

    seg_own = segment_ids
    tok_own = reorder(tokens, places)
    tok_next = reorder(tok_next, places)
    gain_first = blocks_of(mixer_gain.astype(f32), places)[None]
    gain_second = blocks_of(dense_gain.astype(f32), places)
    down = blocks_of(decay_down, places).astype(bf16)
    head = 2 * core + near
    up_own = lax.dynamic_slice_in_dim(decay_up, head * DK, DK, 1).astype(f32)
    bias_own = lax.dynamic_slice_in_dim(decay_bias, head * DK, DK, 0).astype(f32)[None]
    gain_heads = head_gain.astype(f32)[None]

    def root_of(values):
        return lax.rsqrt(jnp.mean(values * values, axis=-1, keepdims=True) + norm_eps)

    def forward_of(tok, seg):
        return mixer_forward(tok, w_first, down, gain_first, seg, up_own, bias_own, gain_heads)

    first_next, low_next, qkv_next, swish_next, scores_next, mixed_next, gated_next = forward_of(tok_next, seg_next)
    first_own, low_own, qkv_own, swish_own, scores_own, mixed_own, gated_own = forward_of(
        after(tok_own, gated_next), seg_own
    )
    branch_next = product_nt(gated_next, w_out)
    branch_ahead = summed_ahead(branch_next)
    branch_own = product_nt(after(gated_own, branch_next), w_out)
    w_g = z_then_y(pair_g, along_g, rest_g, [(gated_own,), (branch_own,), (branch_own,)])
    branch = summed_here(branch_own, branch_ahead)
    hidden = half(tok_own, core).astype(f32) + branch
    root_hidden = root_of(hidden)
    second_half = (hidden * root_hidden * gain_second).astype(bf16)
    w_u = z_then_y(pair_u, along_u, rest_u, [(branch_own,), (second_half,), (second_half,)])
    w_d = y_then_z(pair_d, rest_d)
    second_next = from_neighbour(second_half)
    second_own = whole_chip(second_half)
    cot_own = reorder(after(cotangent, second_half), places)
    cot_next = reorder(after(cot_next, second_half), places)

    gate_own, upper_own, product_own = dense_forward(second_own, w_g, w_u)
    gate_next, upper_next, product_next = dense_forward(after(second_next, product_own), w_g, w_u)
    cots, products, second = (cot_own, cot_next), (product_own, product_next), (second_own, second_next)

    def tied(values, *others):
        return [after(one, *others) for one in values]

    def norm_pull(values, root, gain, wanted):
        scaled = wanted * gain
        return root * scaled - values * (
            root * root * root * jnp.mean(values * scaled, axis=-1, keepdims=True)
        )

    (slab_d,) = slabs(cots, products)
    y_d = sent_y(slab_d)
    d_gate_next, d_up_next, d_second_next = dense_backward(after(cot_next, slab_d), w_d, w_g, w_u, gate_next, upper_next)
    d_gate_own, d_up_own, d_second_own = dense_backward(
        after(cot_own, d_second_next), w_d, w_g, w_u, gate_own, upper_own
    )
    second_ahead = summed_ahead(d_second_next)
    d_gates, d_ups = (d_gate_own, d_gate_next), (d_up_own, d_up_next)
    (slab_g,) = slabs(second, d_gates)
    y_g = sent_y(slab_g)
    (slab_u,) = slabs(second, tied(d_ups, slab_g))
    y_u = sent_y(slab_u)
    d_second = summed_here(d_second_own, after(second_ahead, slab_u))
    d_hidden = half(cot_own, core).astype(f32) + norm_pull(hidden, root_hidden, gain_second, d_second)
    grad_dense_gain = jnp.sum(d_second * hidden * root_hidden, axis=0)
    d_branch_half = d_hidden.astype(bf16)
    d_branch_next = from_neighbour(d_branch_half)
    d_branch_own = whole_chip(d_branch_half)
    fixed_own = (up_own, bias_own, gain_heads)
    d_qkvs_own, d_low_own, d_first_own, *small_own = mixer_backward(
        d_branch_own, w_out, w_first, down, qkv_own, swish_own, low_own, seg_own, *fixed_own, scores_own, mixed_own
    )
    sum_d = own_slab(cots, products, tied(y_d, d_first_own))
    d_qkvs_next, d_low_next, d_first_next, *small_next = mixer_backward(
        after(d_branch_next, sum_d), w_out, w_first, down, qkv_next, swish_next, low_next, seg_next, *fixed_own,
        scores_next, mixed_next,
    )
    firsts, d_parts = (first_own, first_next), (d_qkvs_own, d_qkvs_next)
    (slab_first,) = slabs(firsts, d_parts)
    y_first = sent_y(slab_first)
    d_branches, gateds = (d_branch_own, d_branch_next), (gated_own, gated_next)
    (slab_o,) = slabs(d_branches, tied(gateds, slab_first))
    first_ahead = summed_ahead(after(d_first_next, slab_first))
    sum_g = own_slab(second, d_gates, tied(y_g, slab_o))
    out_d = finish(sum_d)
    out_g = finish(sum_g)
    dense_next = product_nt(after(product_next, sum_g), w_d)
    dense_own = product_nt(after(product_own, dense_next), w_d)
    dense_ahead = summed_ahead(dense_next)
    sum_u = own_slab(second, d_ups, tied(y_u, dense_own))
    out_u = finish(sum_u)
    y_o = sent_y(slab_o)
    d_first = summed_here(d_first_own, first_ahead)
    tok_mine = half(tok_own, core).astype(f32)
    root_mine = root_of(tok_mine)
    grad_half = d_hidden + norm_pull(tok_mine, root_mine, gain_first[0], d_first)
    grad_mixer_gain = jnp.sum(d_first * tok_mine * root_mine, axis=0)
    grad_tokens = reorder(whole_chip(grad_half), back)
    dense_out = summed_here(dense_own, dense_ahead)
    output = reorder(whole_chip((hidden + dense_out).astype(bf16)), back)
    out_first = finish(own_slab(firsts, d_parts, y_first))
    out_o = finish(own_slab(d_branches, gateds, y_o))

    def down_part(first, d_low):
        return lax.dot_general(
            first.astype(f32), d_low, (((0,), (0,)), ((), ())), precision=HIGH, preferred_element_type=f32
        )

    grad_down = down_part(first_own, d_low_own) + down_part(first_next, d_low_next)
    grad_up, grad_bias, grad_head = (one + two for one, two in zip(small_own, small_next))
    small = [
        blocks_of(grad_mixer_gain, back),
        blocks_of(grad_dense_gain, back),
        grad_head[0],
        blocks_of(grad_down, back),
        lax.dynamic_update_slice_in_dim(jnp.zeros(decay_up.shape, f32), grad_up, head * DK, 1),
        lax.dynamic_update_slice_in_dim(jnp.zeros(decay_bias.shape, f32), grad_bias[0], head * DK, 0),
    ]
    packed = jnp.concatenate([one.reshape(-1, 128) for one in small], 0)
    packed = packed + core_swap(packed)
    for axis in (3, 2, 1, 0):
        reach = 1
        while reach < sizes[axis]:
            packed = packed + lax.ppermute(packed, "dp", exchange_pairs(sizes, axis, reach))
            reach *= 2
    places_of = np.cumsum([0] + [one.size // 128 for one in small])
    small = [
        packed[begin:end].reshape(one.shape) for one, begin, end in zip(small, places_of[:-1], places_of[1:])
    ]


    def all_of(parts):
        return columns(parts, 0, parts[0].shape[1])

    return (
        output,
        grad_tokens,
        small[0],
        columns(out_first, 0, DK),
        columns(out_first, DK, 2 * DK),
        columns(out_first, 2 * DK, 2 * DK + DV),
        columns(out_first, 2 * DK + DV, 2 * DK + 2 * DV),
        small[3],
        small[4],
        small[5],
        small[2],
        all_of(out_o).T,
        small[1],
        all_of(out_g),
        all_of(out_u),
        all_of(out_d).T,
    )


def solution(mesh):
    rows, large, turned, whole = P("dp", None), P("dp", "tensor"), P("tensor", "dp"), P()
    in_specs = (
        rows, P("dp"), rows, whole, large, large, large, large, whole, whole, whole, whole, turned,
        whole, large, large, turned,
    )
    out_specs = (
        rows, rows, whole, large, large, large, large, whole, whole, whole, whole, turned, whole,
        large, large, turned,
    )
    return jax.shard_map(on_device, mesh=mesh, in_specs=in_specs, out_specs=out_specs, check_vma=False)
```

```python
from functools import partial
from types import SimpleNamespace

import jax
import jax.numpy as jnp
import numpy as np
from jax import lax
from jax.experimental import pallas as pl
from jax.experimental.pallas import tpu as pltpu
from jax.sharding import PartitionSpec as P

DK = 256
DV = 512
PIECE = 256
norm_eps = 1e-06
head_eps = 1e-05
LEVELS = (1, 2, 4, 8, 16, 32, 64, 128)
f32 = jnp.float32
bf16 = jnp.bfloat16
HIGH = lax.Precision.HIGHEST


def layout(chips):
    return {16: (4, 2, 1, 2), 64: (4, 4, 2, 2)}.get(chips, (1, 1, chips // 2, 2))


def split_place(place, sizes):
    _, deep, far, _ = sizes
    near = lax.rem(place, np.int32(2))
    far_at = lax.rem(lax.div(place, np.int32(2)), np.int32(far))
    y_at = lax.rem(lax.div(place, np.int32(2 * far)), np.int32(deep))
    return lax.div(place, np.int32(2 * far * deep)), y_at, far_at, near


def mm(left, right):
    return lax.dot_general(left, right, (((1,), (0,)), ((), ())), preferred_element_type=f32)


def mm_nt(left, right):
    return lax.dot_general(left, right, (((1,), (1,)), ((), ())), preferred_element_type=f32)


def mm_tn(left, right):
    return lax.dot_general(left, right, (((0,), (0,)), ((), ())), preferred_element_type=f32)


def reorder_kernel(places, source, target):
    count = places.shape[0]
    width = source.shape[1] // count
    for block in range(count):
        start = pl.multiple_of(places[block] * width, width)
        target[:, block * width : (block + 1) * width] = source[:, pl.ds(start, width)]


def reorder(values, places):
    rows, columns = values.shape
    count = places.shape[0]
    width = columns // count
    if width % 128 != 0:
        return jnp.concatenate(
            [lax.dynamic_slice_in_dim(values, places[i] * width, width, 1) for i in range(count)], 1
        )
    tile = 192 if rows % 192 == 0 else rows
    return pl.pallas_call(
        reorder_kernel,
        out_shape=jax.ShapeDtypeStruct(values.shape, values.dtype),
        grid_spec=pltpu.PrefetchScalarGridSpec(
            num_scalar_prefetch=1,
            grid=(rows // tile,),
            in_specs=[pl.BlockSpec((tile, columns), lambda i, p: (i, 0))],
            out_specs=pl.BlockSpec((tile, columns), lambda i, p: (i, 0)),
        ),
        cost_estimate=pl.CostEstimate(
            flops=0, bytes_accessed=2 * values.size * values.dtype.itemsize, transcendentals=0
        ),
        name="reorder",
    )(places, values)


def bit_of(shape, level):
    return (lax.broadcasted_iota(jnp.int32, shape, 0) & level) != 0


def partner(values, level, upper):
    size = values.shape[0]
    return jnp.where(
        upper, pltpu.roll(values, level, 0), pltpu.roll(values, size - level, 0)
    )


def same_document(seg_row):
    across = jnp.broadcast_to(seg_row[0].astype(f32), (PIECE, PIECE))
    return across == across.T


def log_decay(low, up, bias):
    pre = jnp.dot(low, up, precision=HIGH, preferred_element_type=f32) + bias
    return pre, (jnp.minimum(pre, 0.0) - jnp.log1p(jnp.exp(-jnp.abs(pre)))) * (1.0 / 16.0)


def level_exponents(decay):
    prefix, suffix, total = decay, jnp.zeros_like(decay), decay
    found = []
    for level in LEVELS:
        upper = bit_of(decay.shape, level)
        found.append(jnp.where(upper, prefix, suffix))
        if level != LEVELS[-1]:
            beside = partner(total, level, upper)
            prefix = prefix + jnp.where(upper, beside, 0.0)
            suffix = suffix + jnp.where(upper, 0.0, beside)
            total = total + beside
    return found


def pair_distance():
    rows = lax.broadcasted_iota(jnp.int32, (PIECE, PIECE), 0)
    columns = lax.broadcasted_iota(jnp.int32, (PIECE, PIECE), 1)
    return rows ^ columns, rows >= columns


def fixed(shape):
    return pl.BlockSpec(shape, lambda i: (0,) * len(shape), pipeline_mode=pl.Buffered(1))


def by_rows(tile, width):
    return pl.BlockSpec((tile, width), lambda i: (i, 0))


def shape_of(rows, width, kind):
    return jax.ShapeDtypeStruct((rows, width), kind)


vmem_limit = 60 * 1024 * 1024


def piece_attention(query_low, keyset_low, decay):
    query, keyset = query_low.astype(f32), keyset_low.astype(f32)
    apart, causal = pair_distance()
    scores = mm_nt(query_low, keyset_low)
    for level, exponent in zip(LEVELS, level_exponents(decay)):
        upper = bit_of(decay.shape, level)
        scaled = (jnp.where(upper, query, keyset) * jnp.exp(exponent)).astype(bf16)
        scores = jnp.where(apart >= level, mm_nt(scaled, scaled), scores)
    return scores, causal


def mixer_forward_kernel(
    tok, w_first, down, gain_first, seg_row, up, bias, gain,
    first_out, low_out, qkv_out, swish_out, scores_out, mixed_out, gated_out,
):
    rows = tok[...].astype(f32)
    root_rows = lax.rsqrt(jnp.mean(rows * rows, axis=-1, keepdims=True) + norm_eps)
    first = (rows * root_rows * gain_first[...]).astype(bf16)
    first_out[...] = first
    low = mm(first, down[...])
    low_out[...] = low
    qkv = mm(first, w_first[:, : 2 * DK + DV]).astype(bf16)
    qkv_out[...] = qkv
    opened = mm(first, w_first[:, 2 * DK + DV :])
    swish_out[...] = opened
    _, decay = log_decay(low, up[...], bias[...])
    scores, causal = piece_attention(qkv[:, :DK], qkv[:, DK : 2 * DK], decay)
    allowed = causal & same_document(seg_row)
    scores = jnp.where(allowed, scores * (DK**-0.5), 0.0).astype(bf16)
    mixed = mm(scores, qkv[:, 2 * DK :])
    scores_out[...] = scores
    mixed_out[...] = mixed
    root = lax.rsqrt(jnp.mean(mixed * mixed, axis=-1, keepdims=True) + head_eps)
    gated_out[...] = (mixed * root * gain[...] * (opened * jax.nn.sigmoid(opened))).astype(bf16)


def mixer_backward_kernel(
    d_branch, w_out, w_first, down, qkv, swish, low, seg_row, up, bias, gain, scores_in, mixed_in, first,
    d_qkvs, d_first, d_up, d_bias, d_gain, d_down,
):
    query = qkv[:, :DK].astype(f32)
    keyset = qkv[:, DK : 2 * DK].astype(f32)
    values = qkv[:, 2 * DK :]
    pre, decay = log_decay(low[...], up[...], bias[...])
    apart, causal = pair_distance()
    mixed = mixed_in[...]
    root = lax.rsqrt(jnp.mean(mixed * mixed, axis=-1, keepdims=True) + head_eps)
    normed = mixed * root
    opened = swish[...]
    sigma = jax.nn.sigmoid(opened)
    wanted = mm(d_branch[...], w_out[...])
    d_swish = (wanted * normed * gain[...] * (sigma + opened * sigma * (1.0 - sigma))).astype(bf16)
    d_scaled = wanted * (opened * sigma)
    gain_part = jnp.sum(d_scaled * normed, axis=0, keepdims=True)
    d_normed = d_scaled * gain[...]
    d_mixed = root * (d_normed - normed * jnp.mean(d_normed * normed, axis=-1, keepdims=True))
    d_mixed = d_mixed.astype(bf16)
    d_values = mm_tn(scores_in[...], d_mixed).astype(bf16)
    allowed = causal & same_document(seg_row)
    d_scores = jnp.where(allowed, mm_nt(d_mixed, values) * (DK**-0.5), 0.0)
    on_diagonal = jnp.sum(jnp.where(apart == 0, d_scores, 0.0), axis=1, keepdims=True)
    d_query = on_diagonal * keyset
    d_keyset = on_diagonal * query
    both = d_scores + d_scores.T
    exponents = level_exponents(decay)
    d_prefix = d_suffix = d_total = jnp.zeros_like(decay)
    for level, exponent in reversed(list(zip(LEVELS, exponents))):
        upper = bit_of(decay.shape, level)
        if level != LEVELS[-1]:
            d_beside = jnp.where(upper, d_prefix, d_suffix) + d_total
            d_total = d_total + partner(d_beside, level, upper)
        base = jnp.where(upper, query, keyset)
        factor = jnp.exp(exponent)
        scaled = (base * factor).astype(bf16)
        here = jnp.where((apart >= level) & (apart < 2 * level), both, 0.0).astype(bf16)
        d_base = mm(here, scaled) * factor
        d_exponent = d_base * base
        d_query = d_query + jnp.where(upper, d_base, 0.0)
        d_keyset = d_keyset + jnp.where(upper, 0.0, d_base)
        d_prefix = d_prefix + jnp.where(upper, d_exponent, 0.0)
        d_suffix = d_suffix + jnp.where(upper, 0.0, d_exponent)
    d_pre = (d_prefix + d_total) * jax.nn.sigmoid(-pre) * (1.0 / 16.0)
    d_query, d_keyset = d_query.astype(bf16), d_keyset.astype(bf16)
    d_qkvs[:, :DK] = d_query
    d_qkvs[:, DK : 2 * DK] = d_keyset
    d_qkvs[:, 2 * DK : 2 * DK + DV] = d_values
    d_qkvs[:, 2 * DK + DV :] = d_swish
    d_low = lax.dot_general(
        d_pre, up[...], (((1,), (1,)), ((), ())), precision=HIGH, preferred_element_type=f32
    )
    high = d_low.astype(bf16)
    rest = (d_low - high.astype(f32)).astype(bf16)
    d_down[...] += mm_tn(high, first[...]) + mm_tn(rest, first[...])
    d_first[...] = (
        mm_nt(d_query, w_first[:, :DK])
        + mm_nt(d_keyset, w_first[:, DK : 2 * DK])
        + mm_nt(d_values, w_first[:, 2 * DK : 2 * DK + DV])
        + mm_nt(d_swish, w_first[:, 2 * DK + DV :])
        + lax.dot_general(
            d_low, down[...].astype(f32), (((1,), (1,)), ((), ())), precision=HIGH, preferred_element_type=f32
        )
    ).astype(bf16)
    d_up[...] += lax.dot_general(
        low[...], d_pre, (((0,), (0,)), ((), ())), precision=HIGH, preferred_element_type=f32
    )
    d_bias[...] += jnp.sum(d_pre, axis=0, keepdims=True)
    d_gain[...] += gain_part


def dense_forward_kernel(second, w_g, w_u, gate_out, upper_out, product_out):
    gate = mm(second[...], w_g[...])
    gate_out[...] = gate
    upper = mm(second[...], w_u[...])
    upper_out[...] = upper
    product_out[...] = (gate * jax.nn.sigmoid(gate) * upper).astype(bf16)


def dense_backward_kernel(cot, w_d, w_g, w_u, gate_in, upper_in, d_gate_out, d_up_out, d_second):
    gate = gate_in[...]
    sigma = jax.nn.sigmoid(gate)
    d_product = mm(cot[...], w_d[...])
    d_gate = (d_product * upper_in[...] * (sigma + gate * sigma * (1.0 - sigma))).astype(bf16)
    d_up = (d_product * (gate * sigma)).astype(bf16)
    d_gate_out[...] = d_gate
    d_up_out[...] = d_up
    d_second[...] = (mm_nt(d_gate, w_g[...]) + mm_nt(d_up, w_u[...])).astype(bf16)


class Place:
    def __init__(self, sizes):
        self.sizes = sizes
        tall, deep, far, _ = sizes
        place, self.core = lax.axis_index("dp"), lax.axis_index("tensor")
        self.near = place % 2
        self.far_at = (place // 2) % far
        self.y_at = (place // (2 * far)) % deep
        self.z_at = place // (2 * far * deep)
        self.has_above, self.has_below = self.z_at + 1 < tall, self.z_at >= 1
        self.beside = self.device(self.z_at, self.y_at, self.far_at, 1 - self.near, self.core)
        self.other_core = self.device(self.z_at, self.y_at, self.far_at, self.near, 1 - self.core)
        self.above = self.device(self.z_at + 1, self.y_at, self.far_at, self.near, self.core)
        self.below = self.device(self.z_at - 1, self.y_at, self.far_at, self.near, self.core)
        self.shifts = [(fr, yr) for fr in range(far) for yr in range(deep) if fr or yr]

    def device(self, z, y, far_x, near_x, which):
        _, deep, far, _ = self.sizes
        return (((z * deep + y) * far + far_x) * 2 + near_x, which)

    def peer(self, fr, yr):
        _, deep, far, _ = self.sizes
        return self.device(self.z_at, (self.y_at + yr) % deep, (self.far_at + fr) % far, self.near, self.core)

    def block_of(self, slot):
        tall, deep, far, _ = self.sizes
        back_z, back_y, back_far = slot % tall, (slot // tall) % deep, slot // (tall * deep)
        place = (self.z_at + tall - back_z) % tall * deep + (self.y_at + deep - back_y) % deep
        return place * far + (self.far_at + far - back_far) % far

    def greet(self):
        barrier = pltpu.get_barrier_semaphore()

        def signal(who):
            pl.semaphore_signal(barrier, inc=1, device_id=who, device_id_type=pl.DeviceIdType.MESH)

        signal(self.beside)
        signal(self.other_core)
        for fr, yr in self.shifts:
            signal(self.peer(fr, yr))
        tall = self.sizes[0]
        for step_z in range(1, tall):
            signal(self.device((self.z_at + step_z) % tall, self.y_at, self.far_at, self.near, self.core))
        pl.semaphore_wait(barrier, 2 + len(self.shifts) + tall - 1)

    def partners(self):
        tall, deep, far, _ = self.sizes
        found = [self.other_core, self.beside]
        at = (self.z_at, self.y_at, self.far_at)
        for axis, extent in ((2, far), (1, deep), (0, tall)):
            reach = 1
            while reach < extent:
                to = list(at)
                to[axis] = at[axis] + reach - 2 * reach * (at[axis] // reach % 2)
                found.append(self.device(*to, self.near, self.core))
                reach *= 2
        return found


class Copies:
    def __init__(self, send_sem, recv_sem):
        self.send_sem, self.recv_sem, self.used = send_sem, recv_sem, 0

    def make(self, source, target, who):
        index = self.used
        self.used += 1
        return pltpu.make_async_remote_copy(
            src_ref=source, dst_ref=target, send_sem=self.send_sem.at[index], recv_sem=self.recv_sem.at[index],
            device_id=who, device_id_type=pl.DeviceIdType.MESH,
        )


def stream(body, steps, ins, outs):
    pltpu.emit_pipeline(
        body, grid=(steps,),
        in_specs=[pl.BlockSpec(shape, index) for _, shape, index in ins],
        out_specs=[pl.BlockSpec(shape, index) for _, shape, index in outs],
    )(*[one for one, _, _ in ins], *[one for one, _, _ in outs])


def still(i):
    return (0, 0)


def step(i):
    return (i, 0)


def from_tile(first):
    return lambda i: (first + i, 0)


def pull_of(values, gain, wanted):
    root = lax.rsqrt(jnp.mean(values * values, axis=-1, keepdims=True) + norm_eps)
    scaled = wanted * gain
    pulled = root * scaled - values * (root * root * root * jnp.mean(values * scaled, axis=-1, keepdims=True))
    return pulled, jnp.sum(wanted * values * root, axis=0, keepdims=True)


def backward_part(sizes, r, here, copies):
    tall, deep, far, _ = sizes
    core, near, z_at = here.core, here.near, here.z_at
    width = r.cot.shape[1]
    rows = r.cot.shape[0]
    chip_rows = rows // 2
    half_rows = chip_rows // 2
    units = r.product.shape[1]
    tiles = half_rows // 128
    chip_tiles = chip_rows // 256
    outer = deep * far
    size = width // outer // tall
    slab = size * tall
    for total in (r.d_up_acc, r.d_bias_acc, r.d_gain_acc, r.dense_gain_acc, r.mixer_gain_acc, r.d_down_acc):
        total[...] = jnp.zeros_like(total)
    waits = []
    sides = dict(
        d=(r.cot, r.product), g=(r.second, r.d_gate), u=(r.second, r.d_up), f=(r.first, r.d_qkvs),
        o=(r.d_branch, r.gated),
    )
    slab_tile = 256 if slab % 256 == 0 else 128

    def product_slab(group, number, received, target, slabs_of=1):
        left, right = sides[group]
        columns = right.shape[1]
        at = number * slab // slab_tile

        def body(left_ref, right_ref, *rest):
            total = mm_tn(left_ref[...], right_ref[...])
            for other in rest[:-1]:
                total = total + other[...].astype(f32)
            rest[-1][...] = total.astype(bf16)

        stream(
            body, slabs_of * slab // slab_tile,
            [(left, (rows, slab_tile), lambda i: (0, at + i)), (right, (rows, columns), still)]
            + [(one, (slab_tile, columns), step) for one in received],
            [(target, (slab_tile, columns), step)],
        )

    y_copies, z_copies = {}, {}

    def part(ref, index, count):
        return ref.at[pl.ds(index * count, count)]

    def send_slabs(group):
        made = []
        for number in reversed(range(1, outer)):
            fr, yr = number // deep, number % deep
            source, target = (part(getattr(r, name + group), number - 1, slab) for name in ("y_send_", "y_recv_"))
            product_slab(group, number, (), source)
            copy = copies.make(source, target, here.peer((far - fr) % far, (deep - yr) % deep))
            copy.start()
            made.append(copy)
        y_copies[group] = made
        waits.extend(copy.wait_send for copy in made)

    z_first = ("u",)

    def numbers_of(group):
        return range(outer) if group in z_first else (0,)

    def slot_of(group, number, hop, way):
        return (number * (tall - 1) + hop - 1) * 2 + way

    def z_start(group, hop):
        reach = tall - hop
        goes_up, goes_down = z_at + reach < tall, z_at >= reach
        comes_up = here.has_below & (z_at - 1 + reach < tall)
        comes_down = here.has_above & (z_at + 1 >= reach)
        total, sent, received = (getattr(r, name + group) for name in ("sum_", "z_send_", "z_recv_"))
        made = []
        for number in numbers_of(group):
            if hop == 1:
                rising, falling = (part(total, number * tall + at, size) for at in (tall - reach, reach))
            else:
                rising, falling = (part(sent, slot_of(group, number, hop - 1, way), size) for way in (0, 1))
            up = copies.make(rising, part(received, slot_of(group, number, hop, 0), size), here.above)
            down = copies.make(falling, part(received, slot_of(group, number, hop, 1), size), here.below)
            pl.when(goes_up)(up.start)
            pl.when(goes_down)(down.start)
            waits.append(lambda up=up: pl.when(goes_up)(up.wait_send))
            waits.append(lambda down=down: pl.when(goes_down)(down.wait_send))
            made.append((up, down))
        z_copies[group, hop] = made, comes_up, comes_down

    def z_wait(group, hop):
        made, comes_up, comes_down = z_copies[group, hop]
        for up, down in made:
            pl.when(comes_up)(up.wait_recv)
            pl.when(comes_down)(down.wait_recv)

    def own_sum(group):
        for copy in y_copies[group]:
            copy.wait_recv()
        received = getattr(r, "y_recv_" + group)
        product_slab(
            group, 0, [part(received, number - 1, slab) for number in range(1, outer)], getattr(r, "sum_" + group)
        )
        z_start(group, 1)

    def all_slabs(group):
        product_slab(group, 0, (), getattr(r, "sum_" + group), outer)
        z_start(group, 1)

    def z_next(group, hop):
        z_wait(group, hop - 1)
        reach = tall - hop
        total, sent, received = (getattr(r, name + group) for name in ("sum_", "z_send_", "z_recv_"))
        columns = total.shape[1]

        def body(rising, up, falling, down, rising_out, falling_out):
            rising_out[...] = (
                rising[...].astype(f32) + jnp.where(here.has_below, up[...].astype(f32), 0.0)
            ).astype(bf16)
            falling_out[...] = (
                falling[...].astype(f32) + jnp.where(here.has_above, down[...].astype(f32), 0.0)
            ).astype(bf16)

        block = (size, columns)

        def at(index_of):
            return lambda i: (index_of(i), 0)

        stream(
            body, len(numbers_of(group)),
            [
                (total, block, at(lambda i: i * tall + tall - reach)),
                (received, block, at(lambda i: slot_of(group, i, hop - 1, 0))),
                (total, block, at(lambda i: i * tall + reach)),
                (received, block, at(lambda i: slot_of(group, i, hop - 1, 1))),
            ],
            [
                (sent, block, at(lambda i: slot_of(group, i, hop - 1, 0))),
                (sent, block, at(lambda i: slot_of(group, i, hop - 1, 1))),
            ],
        )
        z_start(group, hop)

    def y_last(group):
        z_wait(group, tall - 1)
        total, received, kept = (getattr(r, name + group) for name in ("sum_", "z_recv_", "y_send_"))
        block = (size, total.shape[1])

        def body(own, up, down, into):
            value = own[...].astype(f32) + jnp.where(here.has_below, up[...].astype(f32), 0.0)
            into[...] = (value + jnp.where(here.has_above, down[...].astype(f32), 0.0)).astype(bf16)

        stream(
            body, outer,
            [
                (total, block, lambda i: (i * tall, 0)),
                (received, block, lambda i: (slot_of(group, i, tall - 1, 0), 0)),
                (received, block, lambda i: (slot_of(group, i, tall - 1, 1), 0)),
            ],
            [(kept, block, step)],
        )
        made = []
        for number in range(1, outer):
            fr, yr = number // deep, number % deep
            target = part(getattr(r, "y_recv_" + group), number - 1, size)
            copy = copies.make(
                part(kept, number, size), target, here.peer((far - fr) % far, (deep - yr) % deep)
            )
            copy.start()
            made.append(copy)
        y_copies[group] = made
        waits.extend(copy.wait_send for copy in made)

    def z_finish(group):
        if group in z_first:
            for copy in y_copies[group]:
                copy.wait_recv()
            received = getattr(r, "y_recv_" + group)
            arrays = [part(getattr(r, "y_send_" + group), 0, size)]
            arrays += [part(received, number - 1, size) for number in range(1, outer)]
            counts = [None] * outer
        else:
            z_wait(group, tall - 1)
            received = getattr(r, "z_recv_" + group)
            arrays = [part(getattr(r, "sum_" + group), 0, size)]
            arrays += [part(received, slot_of(group, 0, tall - 1, way), size) for way in (0, 1)]
            counts = [None, here.has_below, here.has_above]
        block = (size // 2, arrays[0].shape[1])
        number_of = len(arrays)

        def body(*both):
            for inputs, into in ((both[:number_of], both[-2]), (both[number_of:-2], both[-1])):
                total = jnp.zeros(block, f32)
                for one, counted in zip(inputs, counts):
                    value = one[...].astype(f32)
                    total = total + (value if counted is None else jnp.where(counted, value, 0.0))
                into[...] = total.astype(into.dtype)

        mine, theirs = (lambda i: (near, 0)), (lambda i: (1 - near, 0))
        crossing = getattr(r, "cross_" + group)
        stream(
            body, 1,
            [(one, block, mine) for one in arrays] + [(one, block, theirs) for one in arrays],
            [(getattr(r, "kept_" + group), block, still), (crossing, block, still)],
        )
        copy = copies.make(crossing, getattr(r, "received_" + group), here.beside)
        copy.start()
        waits.append(copy.wait)

    partners = here.partners()
    exchanges = []

    def small_begin():
        count, _, each = r.by_block.shape
        r.by_block[...] = jnp.zeros_like(r.by_block)
        r.by_head[...] = jnp.zeros_like(r.by_head)
        rank = r.d_up_acc.shape[0]
        for slot in range(count):
            lanes = pl.ds(slot * each, each)
            at = here.block_of(slot)
            r.by_block[at, 0:1, :] = r.mixer_gain_acc[:, lanes]
            r.by_block[at, 1:2, :] = r.dense_gain_acc[:, lanes]
            r.by_block[at, 8 : 8 + rank, :] = r.d_down_acc[:, lanes]
        head = 2 * core + near
        r.by_head[head, 8 : 8 + rank, :] = r.d_up_acc[...]
        r.by_head[head, 0:1, :] = r.d_bias_acc[...]
        r.by_head[0, 1:2, :] = r.d_gain_acc[:, :DK]
        r.by_head[0, 2:3, :] = r.d_gain_acc[:, DK:]

    def small_send():
        index = len(exchanges)
        made = [
            copies.make(own, got.at[index], partners[index])
            for own, got in ((r.by_block, r.got_block), (r.by_head, r.got_head))
        ]
        for copy in made:
            copy.start()
        exchanges.append(made)

    def small_take():
        index = len(exchanges) - 1
        for copy in exchanges[index]:
            copy.wait()
        r.by_block[...] += r.got_block[index]
        r.by_head[...] += r.got_head[index]
        if len(exchanges) < len(partners):
            small_send()
            return True
        return False

    def rows_of(held, start):
        return held.at[pl.ds(pl.multiple_of(start, 128), half_rows)]

    hands, aheads = {}, {}

    def hand(name, following):
        first = (chip_rows if following else 0) + (1 - core) * half_rows
        suffix = "_next" if following else "_own"
        copy = copies.make(rows_of(getattr(r, name), first), getattr(r, "hand_" + name + suffix), here.other_core)
        copy.start()
        hands[name, following] = copy
        waits.append(copy.wait_send)

    def ahead(name):
        hands[name, True].wait_recv()

        def body(one, other, out):
            out[...] = (one[...].astype(f32) + other[...].astype(f32)).astype(bf16)

        block = (128, width)
        stream(
            body, tiles,
            [(getattr(r, name), block, from_tile(2 * tiles + core * tiles)), (getattr(r, "hand_" + name + "_next"), block, step)],
            [(getattr(r, "ahead_" + name), block, step)],
        )
        copy = copies.make(getattr(r, "ahead_" + name), getattr(r, "behind_" + name), here.beside)
        copy.start()
        aheads[name] = copy
        waits.append(copy.wait_send)

    def summed_inputs(name):
        hands[name, False].wait_recv()
        aheads[name].wait_recv()
        block = (128, width)
        return [
            (getattr(r, name), block, from_tile(core * tiles)), (getattr(r, "hand_" + name + "_own"), block, step),
            (getattr(r, "behind_" + name), block, step),
        ]

    def total_of(one, two, three):
        return one[...].astype(f32) + two[...].astype(f32) + three[...].astype(f32)

    def dense_back(first_tile):
        def body(cot, gate, upper, d_gate, d_up, d_second):
            dense_backward_kernel(
                cot, r.v_w_d, r.v_w_g, r.v_w_u, gate, upper, d_gate, d_up, d_second
            )

        at = from_tile(first_tile)
        stream(
            body, chip_tiles,
            [(r.cot, (256, width), at), (r.gate, (256, units), at), (r.upper, (256, units), at)],
            [(r.d_gate, (256, units), at), (r.d_up, (256, units), at), (r.d_second, (256, width), at)],
        )

    def mixer_back(first_tile):
        def body(d_branch, qkv, swish, low, seg_row, scores, mixed, first, d_qkvs, d_first):
            mixer_backward_kernel(
                d_branch, r.v_w_out, r.v_w_first, r.down, qkv, swish, low, seg_row, r.up,
                r.bias, r.gain_heads, scores, mixed, first, d_qkvs, d_first, r.d_up_acc, r.d_bias_acc,
                r.d_gain_acc, r.d_down_acc,
            )

        at = from_tile(first_tile)

        def whole(held):
            return (held, (PIECE, held.shape[1]), at)

        stream(
            body, chip_rows // PIECE,
            [
                whole(r.d_branch), whole(r.qkv), whole(r.swish), whole(r.low),
                (r.seg_row, (1, 1, PIECE), lambda i: (first_tile + i, 0, 0)), whole(r.scores), whole(r.mixed),
                whole(r.first),
            ],
            [whole(r.d_qkvs), whole(r.d_first)],
        )

    block = (128, width)
    own_half = from_tile(core * tiles)

    send_slabs("d")
    yield
    dense_back(chip_tiles)
    hand("d_second", True)
    dense_back(0)
    hand("d_second", False)
    ahead("d_second")
    send_slabs("g")
    all_slabs("u")

    def dense_out_body(product, out):
        out[...] = mm_nt(product[...], r.v_w_d[...]).astype(bf16)

    stream(
        dense_out_body, 2 * chip_tiles, [(r.product, (256, units), step)], [(r.dense, (256, width), step)]
    )

    def hidden_body(one, two, three, cot, hidden, d_hidden, d_branch):
        wanted = total_of(one, two, three)
        pulled, gain_part = pull_of(hidden[...], r.gain_second[...], wanted)
        total = cot[...].astype(f32) + pulled
        d_hidden[...] = total
        d_branch[...] = total.astype(bf16)
        r.dense_gain_acc[...] += gain_part

    stream(
        hidden_body, tiles,
        summed_inputs("d_second") + [(r.cot, block, own_half), (r.hidden, block, step)],
        [(r.d_hidden, block, step), (r.d_branch, block, own_half)],
    )
    mine = rows_of(r.d_branch, core * half_rows)
    there = rows_of(r.d_branch, chip_rows + core * half_rows)
    share_branch = copies.make(mine, mine, here.other_core)
    cross_branch = copies.make(mine, there, here.beside)
    share_branch.start()
    cross_branch.start()
    waits.extend([share_branch.wait_send, cross_branch.wait_send])
    hand("dense", True)
    hand("dense", False)
    share_branch.wait_recv()
    z_next("u", 2)
    mixer_back(0)
    hand("d_first", False)
    cross_branch.wait_recv()
    share_next = copies.make(there, there, here.other_core)
    share_next.start()
    waits.append(share_next.wait_send)
    own_sum("d")
    z_next("u", 3)
    share_next.wait_recv()
    mixer_back(chip_tiles)
    hand("d_first", True)
    send_slabs("f")
    ahead("d_first")
    y_last("u")
    send_slabs("o")
    own_sum("g")
    z_next("d", 2)
    ahead("dense")
    z_next("g", 2)
    z_next("d", 3)

    def tokens_body(one, two, three, d_hidden, tok, out):
        wanted = total_of(one, two, three)
        pulled, gain_part = pull_of(tok[...].astype(f32), r.gain_first[...], wanted)
        out[...] = d_hidden[...] + pulled
        r.mixer_gain_acc[...] += gain_part

    stream(
        tokens_body, tiles,
        summed_inputs("d_first") + [(r.d_hidden, block, step), (r.tok, block, own_half)],
        [(r.grad_tokens, block, own_half)],
    )
    mine = rows_of(r.grad_tokens, core * half_rows)
    copy = copies.make(mine, mine, here.other_core)
    copy.start()
    waits.append(copy.wait)
    small_begin()
    small_send()
    z_next("g", 3)

    def output_body(one, two, three, hidden, out):
        out[...] = (hidden[...] + total_of(one, two, three)).astype(bf16)

    stream(
        output_body, tiles, summed_inputs("dense") + [(r.hidden, block, step)], [(r.output, block, own_half)]
    )
    mine = rows_of(r.output, core * half_rows)
    copy = copies.make(mine, mine, here.other_core)
    copy.start()
    waits.append(copy.wait)
    small_take()
    z_finish("u")
    z_finish("d")
    small_take()
    z_finish("g")
    own_sum("f")
    own_sum("o")
    small_take()
    z_next("f", 2)
    z_next("o", 2)
    small_take()
    z_next("f", 3)
    z_next("o", 3)
    while small_take():
        pass
    z_finish("f")
    z_finish("o")
    yield
    for wait in waits:
        wait()


def forward_part(sizes, r, here, copies):
    tall, deep, far, _ = sizes
    core, near, z_at = here.core, here.near, here.z_at
    first, out, gate, up, down = range(5)
    weights = (r.w_first, r.w_out, r.w_g, r.w_u, r.w_d)
    shards = {
        first: (r.s_query, r.s_key, r.s_value, r.s_swish), out: (r.s_output,), gate: (r.s_gate,), up: (r.s_up,),
        down: (r.s_down,),
    }
    chip_rows, width = r.tokens.shape
    half_rows = chip_rows // 2
    tiles, chip_tiles, pieces = half_rows // 128, chip_rows // 256, chip_rows // PIECE
    outer = deep * far
    block = r.s_query.shape[0]
    size = 2 * block
    units = r.w_g.shape[1]
    waits, locals_made, loads = [], {}, {}

    def local(source, target):
        index = len(locals_made)
        locals_made[index] = copy = pltpu.make_async_copy(source, target, r.load_sem.at[index])
        copy.start()
        return copy

    def load(source, target):
        loads[source] = local(weights[source], target)

    crossings = {}

    def cross(group):
        mine = pl.ds(pl.multiple_of(near * block, 16), block)
        made, at = [], 0
        for shard in shards[group]:
            columns = shard.shape[1] // 2
            there = pl.ds(at, columns)
            keep = shard.at[:, pl.ds(pl.multiple_of(near * columns, 128), columns)]
            give = shard.at[:, pl.ds(pl.multiple_of((1 - near) * columns, 128), columns)]
            target = weights[group].at[mine, there]
            remote = copies.make(give, target, here.beside)
            remote.start()
            made.append((local(keep, target), remote))
            waits.append(remote.wait_send)
            at += columns
        crossings[group] = made

    def arrive(group):
        for kept, remote in crossings[group]:
            kept.wait()
            remote.wait_recv()

    def slab(group, number, back):
        return weights[group].at[pl.ds((number * tall + back) * size, size)]

    sideways = {}

    def spread(group, back, condition=None):
        for number, (fr, yr) in enumerate(here.shifts):
            key = (group, number, back)
            if key not in sideways:
                sideways[key] = copies.make(
                    slab(group, 0, back), slab(group, number + 1, back), here.peer(fr, yr)
                )
            if condition is None:
                sideways[key].start()
            else:
                pl.when(condition)(sideways[key].start)

    def sides_done(group, backs):
        for number in range(outer - 1):
            for back in backs:
                sideways[group, number, back].wait()

    along = {}

    def hop_start(group, hop, numbers=(0,)):
        rises, falls = here.has_above & (z_at >= hop - 1), here.has_below & (z_at + hop - 1 < tall)
        made = []
        for number in numbers:
            rising = copies.make(slab(group, number, hop - 1), slab(group, number, hop), here.above)
            falling = copies.make(
                slab(group, number, (tall - hop + 1) % tall), slab(group, number, tall - hop), here.below
            )
            pl.when(rises)(rising.start)
            pl.when(falls)(falling.start)
            waits.append(lambda rising=rising: pl.when(rises)(rising.wait_send))
            waits.append(lambda falling=falling: pl.when(falls)(falling.wait_send))
            made.append((rising, falling))
        along[group, hop] = made

    def hop_take(group, hop, sideways_too=True, numbers=(0,)):
        came_up, came_down = z_at >= hop, z_at + hop < tall
        for rising, falling in along[group, hop]:
            pl.when(came_up)(rising.wait_recv)
            pl.when(came_down)(falling.wait_recv)
        if hop + 1 < tall:
            hop_start(group, hop + 1, numbers)
        if sideways_too:
            spread(group, hop, came_up)
            spread(group, tall - hop, came_down)

    def rows_of(rows, start):
        return rows.at[pl.ds(pl.multiple_of(start, 128), half_rows)]

    def give_rows(held):
        copy = copies.make(
            rows_of(held, core * half_rows), rows_of(held, chip_rows + core * half_rows), here.beside
        )
        copy.start()
        waits.append(copy.wait_send)
        return copy

    def share_rows(held, start):
        rows = rows_of(held, start + core * half_rows)
        copy = copies.make(rows, rows, here.other_core)
        copy.start()
        waits.append(copy.wait_send)
        return copy

    def reordered(source, target):
        count = outer * tall
        each = width // count

        def body(one, into):
            for slot in range(count):
                place = here.block_of(slot)
                held = one[:, pl.ds(pl.multiple_of(place * each, each), each)] if each % 128 == 0 else None
                into[:, slot * each : (slot + 1) * each] = (
                    one[:, slot * each : (slot + 1) * each] if held is None else held
                )

        stream(
            body, chip_rows // 128, [(source, (128, width), step)], [(target, (128, width), step)]
        )

    def mixer(first_tile):
        def body(tok, seg_row, first_out, low, qkv, swish, scores, mixed, gated):
            mixer_forward_kernel(
                tok, r.v_w_first, r.down, r.gain_first, seg_row, r.up, r.bias, r.gain_heads,
                first_out, low, qkv, swish, scores, mixed, gated,
            )

        at = from_tile(first_tile)

        def whole(held):
            return (held, (PIECE, held.shape[1]), at)

        stream(
            body, pieces, [whole(r.tok), (r.seg_row, (1, 1, PIECE), lambda i: (first_tile + i, 0, 0))],
            [whole(held) for held in (r.first, r.low, r.qkv, r.swish, r.scores, r.mixed, r.gated)],
        )

    def branch_product(first_tile):
        def body(gated, into):
            into[...] = mm_nt(gated[...], r.v_w_out[...]).astype(bf16)

        at = from_tile(first_tile)
        stream(body, chip_tiles, [(r.gated, (256, DV), at)], [(r.branch, (256, width), at)])

    def hand(following):
        start = (chip_rows if following else 0) + (1 - core) * half_rows
        target = r.hand_next if following else r.hand_own
        copy = copies.make(rows_of(r.branch, start), target, here.other_core)
        copy.start()
        waits.append(copy.wait_send)
        return copy

    def dense(first_tile):
        def body(second, gate_out, upper, product):
            dense_forward_kernel(second, r.v_w_g, r.v_w_u, gate_out, upper, product)

        at = from_tile(first_tile)
        stream(
            body, chip_tiles, [(r.second, (256, width), at)],
            [(held, (256, units), at) for held in (r.gate, r.upper, r.product)],
        )

    row_block = (128, width)
    own_half = from_tile(core * tiles)
    everywhere = range(outer)

    cross(first)
    reordered(r.tokens, r.tok)
    seg_own = local(r.seg_in, r.seg_row.at[pl.ds(0, pieces)])
    arrive(first)
    hop_start(first, 1)
    spread(first, 0)
    for group in (out, gate, up, down):
        cross(group)
    seg_cross = copies.make(r.seg_in, r.seg_row.at[pl.ds(pieces, pieces)], here.beside)
    seg_cross.start()
    waits.append(seg_cross.wait_send)
    tok_cross = give_rows(r.tok)
    reordered(r.cotangent, r.cot)
    cot_cross = give_rows(r.cot)
    arrive(out)
    spread(out, 0)
    hop_take(first, 1)
    hop_take(first, 2) if tall > 2 else None
    hop_start(out, 1)
    arrive(gate)
    spread(gate, 0)
    for hop in range(3, tall):
        hop_take(first, hop)
    hop_start(gate, 1)
    tok_cross.wait_recv()
    tok_share = share_rows(r.tok, chip_rows)
    for hop in range(1, tall):
        hop_take(out, hop)
    arrive(up)
    arrive(down)
    sides_done(first, range(tall))
    load(first, r.v_w_first)
    spread(down, 0)
    spread(up, 0)
    seg_own.wait()
    seg_cross.wait_recv()
    tok_share.wait_recv()
    loads[first].wait()
    hop_take(gate, 1)
    mixer(pieces)
    hop_take(gate, 2) if tall > 2 else None
    sides_done(out, range(tall))
    load(out, r.v_w_out)
    hop_start(up, 1)
    loads[out].wait()
    branch_product(chip_tiles)
    hand_next = hand(True)
    mixer(0)
    for hop in range(3, tall):
        hop_take(gate, hop)
    hop_take(up, 1)
    branch_product(0)
    hand_own = hand(False)
    hand_next.wait_recv()

    def ahead_body(one, other, into):
        into[...] = (one[...].astype(f32) + other[...].astype(f32)).astype(bf16)

    stream(
        ahead_body, tiles,
        [(r.branch, row_block, from_tile(2 * tiles + core * tiles)), (r.hand_next, row_block, step)],
        [(r.ahead, row_block, step)],
    )
    ahead = copies.make(r.ahead, r.behind, here.beside)
    ahead.start()
    waits.append(ahead.wait_send)
    cot_cross.wait_recv()
    cot_share = share_rows(r.cot, chip_rows)
    for hop in range(2, tall):
        hop_take(up, hop)
    sides_done(down, (0,))
    hop_start(down, 1, everywhere)
    hand_own.wait_recv()
    ahead.wait_recv()

    def hidden_body(one, two, three, tok, hidden_out, second_out):
        hidden = tok[...].astype(f32) + (
            one[...].astype(f32) + two[...].astype(f32) + three[...].astype(f32)
        )
        hidden_out[...] = hidden
        root = lax.rsqrt(jnp.mean(hidden * hidden, axis=-1, keepdims=True) + norm_eps)
        second_out[...] = (hidden * root * r.gain_second[...]).astype(bf16)

    stream(
        hidden_body, tiles,
        [
            (r.branch, row_block, own_half), (r.hand_own, row_block, step), (r.behind, row_block, step),
            (r.tok, row_block, own_half),
        ],
        [(r.hidden, row_block, step), (r.second, row_block, own_half)],
    )
    second_share = share_rows(r.second, 0)
    second_cross = give_rows(r.second)
    sides_done(gate, range(tall))
    load(gate, r.v_w_g)
    second_cross.wait_recv()
    second_next = share_rows(r.second, chip_rows)
    hop_take(down, 1, False, everywhere)
    sides_done(up, range(tall))
    load(up, r.v_w_u)
    second_share.wait_recv()
    loads[gate].wait()
    loads[up].wait()
    dense(0)
    if tall > 2:
        hop_take(down, 2, False, everywhere)
    second_next.wait_recv()
    dense(chip_tiles)
    cot_share.wait_recv()
    yield
    for hop in range(3, tall):
        hop_take(down, hop, False, everywhere)
    load(down, r.v_w_d)
    loads[down].wait()
    yield
    for wait in waits:
        wait()


def layer_kernel(sizes, names, *refs):
    r = SimpleNamespace(**dict(zip(names, refs)))
    here = Place(sizes)
    here.greet()
    copies = Copies(r.send_sem, r.recv_sem)
    fore, back = forward_part(sizes, r, here, copies), backward_part(sizes, r, here, copies)
    next(fore)
    next(back)
    next(fore)
    next(back)
    for part in (fore, back):
        for _ in part:
            pass


def layer(sizes, small, large):
    tall, deep, far, _ = sizes
    chip_rows, width = large["tokens"].shape
    rows, half_rows = 2 * chip_rows, chip_rows // 2
    pieces = rows // PIECE
    units = large["s_gate"].shape[1] // 2
    rank = small["down"].shape[1]
    qkvs = 2 * DK + 2 * DV
    outer = deep * far
    count = outer * tall
    size = width // count
    slab = size * tall
    outs = dict(
        w_first=(width, qkvs), w_out=(width, DV), w_g=(width, units), w_u=(width, units), w_d=(width, units),
        tok=(rows, width), cot=(rows, width), first=(rows, width), low=(rows, rank, f32), qkv=(rows, 2 * DK + DV),
        swish=(rows, DV, f32), scores=(rows, PIECE), mixed=(rows, DV, f32), gated=(rows, DV),
        hidden=(half_rows, width, f32), second=(rows, width), gate=(rows, units, f32), upper=(rows, units, f32),
        product=(rows, units), branch=(rows, width), hand_next=(half_rows, width), hand_own=(half_rows, width),
        ahead=(half_rows, width), behind=(half_rows, width), d_gate=(rows, units), d_up=(rows, units),
        d_qkvs=(rows, qkvs), d_branch=(rows, width), d_hidden=(half_rows, width, f32), d_second=(rows, width),
        dense=(rows, width), d_first=(rows, width), grad_tokens=(chip_rows, width, f32), output=(chip_rows, width),
    )
    for name in ("d_second", "dense", "d_first"):
        for kind in ("hand_" + name + "_next", "hand_" + name + "_own", "ahead_" + name, "behind_" + name):
            outs[kind] = (half_rows, width)
    for group, columns in dict(d=units, g=units, u=units, f=qkvs, o=DV).items():
        numbers = outer if group == "u" else 1
        outs["kept_" + group] = (size // 2, columns, f32)
        outs["received_" + group] = outs["cross_" + group] = (size // 2, columns)
        outs["sum_" + group] = (numbers * slab, columns)
        outs["y_send_" + group] = (outer * size if group == "u" else (outer - 1) * slab, columns)
        outs["y_recv_" + group] = ((outer - 1) * (size if group == "u" else slab), columns)
        outs["z_send_" + group] = outs["z_recv_" + group] = (numbers * 2 * (tall - 1) * size, columns)
    shapes = {
        name: jax.ShapeDtypeStruct(one[:2], one[2] if len(one) > 2 else bf16) for name, one in outs.items()
    }
    shapes.update(seg_row=jax.ShapeDtypeStruct((pieces, 1, PIECE), jnp.int32))
    heads = large["s_query"].shape[1] * 2 // DK
    inner = dict(
        by_block=jax.ShapeDtypeStruct((count, 8 + rank, size), f32),
        by_head=jax.ShapeDtypeStruct((heads, 8 + rank, DK), f32),
    )
    steps = 2 + int(np.log2(count))
    vmem = pltpu.VMEM
    scratch = dict(
        d_up_acc=vmem((rank, DK), f32), d_bias_acc=vmem((1, DK), f32), d_gain_acc=vmem((1, DV), f32),
        dense_gain_acc=vmem((1, width), f32), mixer_gain_acc=vmem((1, width), f32),
        d_down_acc=vmem((rank, width), f32), got_block=vmem((steps, count, 8 + rank, size), f32),
        got_head=vmem((steps, heads, 8 + rank, DK), f32),
        v_w_first=vmem((width, qkvs), bf16), v_w_out=vmem((width, DV), bf16), v_w_g=vmem((width, units), bf16),
        v_w_u=vmem((width, units), bf16), v_w_d=vmem((width, units), bf16),
    )
    transfers = 8 + 5 * (outer - 1) * tall + (4 + outer) * 2 * (tall - 1) + 12
    transfers += 5 * (outer - 1 + 1) + (4 + outer) * 2 * (tall - 1) + 16 + 2 * steps
    scratch.update(
        load_sem=pltpu.SemaphoreType.DMA((15,)), send_sem=pltpu.SemaphoreType.DMA((transfers,)),
        recv_sem=pltpu.SemaphoreType.DMA((transfers,)),
    )
    anywhere, inside = pl.BlockSpec(memory_space=pl.ANY), pl.BlockSpec(memory_space=vmem)
    names = (*small, *large, *shapes, *inner, *scratch)
    results = pl.pallas_call(
        partial(layer_kernel, sizes, names),
        in_specs=[inside] * len(small) + [anywhere] * len(large),
        out_specs=[anywhere] * len(shapes) + [inside] * len(inner),
        out_shape=[*shapes.values(), *inner.values()],
        scratch_shapes=list(scratch.values()),
        compiler_params=pltpu.CompilerParams(
            collective_id=0, has_side_effects=True, vmem_limit_bytes=vmem_limit
        ),
        cost_estimate=pl.CostEstimate(flops=1, bytes_accessed=1, transcendentals=0),
        name="layer",
    )(*small.values(), *large.values())
    return SimpleNamespace(**dict(zip((*shapes, *inner), results)))


def on_device(
    tokens, segment_ids, cotangent, mixer_gain, w_query, w_key, w_value, w_swish, decay_down, decay_up,
    decay_bias, head_gain, w_output, dense_gain, w_gate, w_up, w_down,
):
    sizes = layout(lax.axis_size("dp"))
    tall, deep, far, _ = sizes
    core = lax.axis_index("tensor")
    place = lax.axis_index("dp")
    z_at, y_at, far_at, near = split_place(place, sizes)
    own_rows = tokens.shape[0]
    half_rows = own_rows // 2
    width = tokens.shape[1]
    block = width // lax.axis_size("dp")

    count = tall * deep * far
    slot = np.arange(count, dtype=np.int32)
    slot_z, slot_y, slot_far = slot % tall, (slot // tall) % deep, slot // (tall * deep)
    from_z, from_y, from_far = slot // (deep * far), (slot // far) % deep, slot % far

    def counted(at, backwards, size):
        return lax.rem(at + (size - backwards), np.int32(size))

    places = (counted(z_at, slot_z, tall) * deep + counted(y_at, slot_y, deep)) * far + counted(far_at, slot_far, far)
    back = (counted(far_at, from_far, far) * deep + counted(y_at, from_y, deep)) * tall + counted(z_at, from_z, tall)

    def blocks_of(values, order):
        chosen = (order[:, None] == slot[None, :]).astype(f32)
        flat = values.astype(f32).reshape(count, -1)
        return jnp.dot(chosen, flat, precision=HIGH).reshape(values.shape)

    def columns(parts, begin, end):
        own, received = (part[:, begin:end].astype(f32) for part in parts)
        return jnp.where(
            near == 0, jnp.concatenate([own, received], 1), jnp.concatenate([received, own], 1)
        )

    gain_first = blocks_of(mixer_gain.astype(f32), places)[None]
    gain_second = blocks_of(dense_gain.astype(f32), places)[None]
    down = blocks_of(decay_down, places).astype(bf16)
    head = 2 * core + near
    up_own = lax.dynamic_slice_in_dim(decay_up, head * DK, DK, 1).astype(f32)
    bias_own = lax.dynamic_slice_in_dim(decay_bias, head * DK, DK, 0).astype(f32)[None]
    gain_heads = head_gain.astype(f32)[None]

    aligned = (width // count) % 128 == 0
    small = dict(
        up=up_own, bias=bias_own, gain_heads=gain_heads, gain_first=gain_first, gain_second=gain_second, down=down
    )
    made = layer(sizes, small, dict(
        tokens=tokens if aligned else reorder(tokens, places),
        cotangent=cotangent if aligned else reorder(cotangent, places),
        seg_in=segment_ids.reshape(own_rows // PIECE, 1, PIECE), s_query=w_query, s_key=w_key, s_value=w_value,
        s_swish=w_swish, s_output=w_output.T, s_gate=w_gate, s_up=w_up, s_down=w_down.T,
    ))
    output = reorder(made.output, back)
    grad_tokens = reorder(made.grad_tokens, back)
    rank = decay_down.shape[1]
    grad_down = made.by_block[:, 8:].transpose(0, 2, 1).reshape(width, rank)
    small = (
        made.by_block[:, 0].reshape(width), made.by_block[:, 1].reshape(width), made.by_head[0, 1:3].reshape(DV),
        grad_down, made.by_head[:, 8:].transpose(1, 0, 2).reshape(rank, -1), made.by_head[:, 0].reshape(-1),
    )
    out_first, out_o, out_g, out_u, out_d = (
        (made.kept_f, made.received_f), (made.kept_o, made.received_o), (made.kept_g, made.received_g),
        (made.kept_u, made.received_u), (made.kept_d, made.received_d),
    )

    def all_of(parts):
        return columns(parts, 0, parts[0].shape[1])

    return (
        output,
        grad_tokens,
        small[0],
        columns(out_first, 0, DK),
        columns(out_first, DK, 2 * DK),
        columns(out_first, 2 * DK, 2 * DK + DV),
        columns(out_first, 2 * DK + DV, 2 * DK + 2 * DV),
        small[3],
        small[4],
        small[5],
        small[2],
        all_of(out_o).T,
        small[1],
        all_of(out_g),
        all_of(out_u),
        all_of(out_d).T,
    )


def solution(mesh):
    rows, large, turned, whole = P("dp", None), P("dp", "tensor"), P("tensor", "dp"), P()
    in_specs = (
        rows, P("dp"), rows, whole, large, large, large, large, whole, whole, whole, whole, turned,
        whole, large, large, turned,
    )
    out_specs = (
        rows, rows, whole, large, large, large, large, whole, whole, whole, whole, turned, whole,
        large, large, turned,
    )
    return jax.shard_map(on_device, mesh=mesh, in_specs=in_specs, out_specs=out_specs, check_vma=False)
```

```python
from functools import partial
from types import SimpleNamespace

import jax
import jax.numpy as jnp
import numpy as np
from jax import lax
from jax.experimental import pallas as pl
from jax.experimental.pallas import tpu as pltpu
from jax.sharding import PartitionSpec as P

DK = 256
DV = 512
PIECE = 256
norm_eps = 1e-06
head_eps = 1e-05
LEVELS = (1, 2, 4, 8, 16, 32, 64, 128)
f32 = jnp.float32
bf16 = jnp.bfloat16
HIGH = lax.Precision.HIGHEST


def layout(chips):
    return {16: (4, 2, 1, 2), 64: (4, 4, 2, 2)}.get(chips, (1, 1, chips // 2, 2))


def split_place(place, sizes):
    _, deep, far, _ = sizes
    near = lax.rem(place, np.int32(2))
    far_at = lax.rem(lax.div(place, np.int32(2)), np.int32(far))
    y_at = lax.rem(lax.div(place, np.int32(2 * far)), np.int32(deep))
    return lax.div(place, np.int32(2 * far * deep)), y_at, far_at, near


def mm(left, right):
    return lax.dot_general(left, right, (((1,), (0,)), ((), ())), preferred_element_type=f32)


def mm_nt(left, right):
    return lax.dot_general(left, right, (((1,), (1,)), ((), ())), preferred_element_type=f32)


def mm_tn(left, right):
    return lax.dot_general(left, right, (((0,), (0,)), ((), ())), preferred_element_type=f32)


def reorder_kernel(places, source, target):
    count = places.shape[0]
    width = source.shape[1] // count
    for block in range(count):
        start = pl.multiple_of(places[block] * width, width)
        target[:, block * width : (block + 1) * width] = source[:, pl.ds(start, width)]


def reorder(values, places):
    rows, columns = values.shape
    count = places.shape[0]
    width = columns // count
    if width % 128 != 0:
        return jnp.concatenate(
            [lax.dynamic_slice_in_dim(values, places[i] * width, width, 1) for i in range(count)], 1
        )
    tile = 192 if rows % 192 == 0 else rows
    return pl.pallas_call(
        reorder_kernel,
        out_shape=jax.ShapeDtypeStruct(values.shape, values.dtype),
        grid_spec=pltpu.PrefetchScalarGridSpec(
            num_scalar_prefetch=1,
            grid=(rows // tile,),
            in_specs=[pl.BlockSpec((tile, columns), lambda i, p: (i, 0))],
            out_specs=pl.BlockSpec((tile, columns), lambda i, p: (i, 0)),
        ),
        cost_estimate=pl.CostEstimate(
            flops=0, bytes_accessed=2 * values.size * values.dtype.itemsize, transcendentals=0
        ),
        name="reorder",
    )(places, values)


def bit_of(shape, level):
    return (lax.broadcasted_iota(jnp.int32, shape, 0) & level) != 0


def partner(values, level, upper):
    size = values.shape[0]
    return jnp.where(
        upper, pltpu.roll(values, level, 0), pltpu.roll(values, size - level, 0)
    )


def same_document(seg_row):
    across = jnp.broadcast_to(seg_row[0].astype(f32), (PIECE, PIECE))
    return across == across.T


def log_decay(low, up, bias):
    pre = jnp.dot(low, up, precision=HIGH, preferred_element_type=f32) + bias
    return pre, (jnp.minimum(pre, 0.0) - jnp.log1p(jnp.exp(-jnp.abs(pre)))) * (1.0 / 16.0)


def level_exponents(decay):
    prefix, suffix, total = decay, jnp.zeros_like(decay), decay
    found = []
    for level in LEVELS:
        upper = bit_of(decay.shape, level)
        found.append(jnp.where(upper, prefix, suffix))
        if level != LEVELS[-1]:
            beside = partner(total, level, upper)
            prefix = prefix + jnp.where(upper, beside, 0.0)
            suffix = suffix + jnp.where(upper, 0.0, beside)
            total = total + beside
    return found


def pair_distance():
    rows = lax.broadcasted_iota(jnp.int32, (PIECE, PIECE), 0)
    columns = lax.broadcasted_iota(jnp.int32, (PIECE, PIECE), 1)
    return rows ^ columns, rows >= columns


def fixed(shape):
    return pl.BlockSpec(shape, lambda i: (0,) * len(shape), pipeline_mode=pl.Buffered(1))


def by_rows(tile, width):
    return pl.BlockSpec((tile, width), lambda i: (i, 0))


def shape_of(rows, width, kind):
    return jax.ShapeDtypeStruct((rows, width), kind)


vmem_limit = 60 * 1024 * 1024


def piece_attention(query_low, keyset_low, decay):
    query, keyset = query_low.astype(f32), keyset_low.astype(f32)
    apart, causal = pair_distance()
    scores = mm_nt(query_low, keyset_low)
    for level, exponent in zip(LEVELS, level_exponents(decay)):
        upper = bit_of(decay.shape, level)
        scaled = (jnp.where(upper, query, keyset) * jnp.exp(exponent)).astype(bf16)
        scores = jnp.where(apart >= level, mm_nt(scaled, scaled), scores)
    return scores, causal


def mixer_forward_kernel(
    tok, w_first, down, gain_first, seg_row, up, bias, gain,
    first_out, low_out, qkv_out, swish_out, scores_out, mixed_out, gated_out,
):
    rows = tok[...].astype(f32)
    root_rows = lax.rsqrt(jnp.mean(rows * rows, axis=-1, keepdims=True) + norm_eps)
    first = (rows * root_rows * gain_first[...]).astype(bf16)
    first_out[...] = first
    low = mm(first, down[...])
    low_out[...] = low
    qkv = mm(first, w_first[:, : 2 * DK + DV]).astype(bf16)
    qkv_out[...] = qkv
    opened = mm(first, w_first[:, 2 * DK + DV :])
    swish_out[...] = opened
    _, decay = log_decay(low, up[...], bias[...])
    scores, causal = piece_attention(qkv[:, :DK], qkv[:, DK : 2 * DK], decay)
    allowed = causal & same_document(seg_row)
    scores = jnp.where(allowed, scores * (DK**-0.5), 0.0).astype(bf16)
    mixed = mm(scores, qkv[:, 2 * DK :])
    scores_out[...] = scores
    mixed_out[...] = mixed
    root = lax.rsqrt(jnp.mean(mixed * mixed, axis=-1, keepdims=True) + head_eps)
    gated_out[...] = (mixed * root * gain[...] * (opened * jax.nn.sigmoid(opened))).astype(bf16)


def mixer_backward_kernel(
    d_branch, w_out, w_first, down, qkv, swish, low, seg_row, up, bias, gain, scores_in, mixed_in, first,
    d_qkvs, d_first, d_up, d_bias, d_gain, d_down,
):
    query = qkv[:, :DK].astype(f32)
    keyset = qkv[:, DK : 2 * DK].astype(f32)
    values = qkv[:, 2 * DK :]
    pre, decay = log_decay(low[...], up[...], bias[...])
    apart, causal = pair_distance()
    mixed = mixed_in[...]
    root = lax.rsqrt(jnp.mean(mixed * mixed, axis=-1, keepdims=True) + head_eps)
    normed = mixed * root
    opened = swish[...]
    sigma = jax.nn.sigmoid(opened)
    wanted = mm(d_branch[...], w_out[...])
    d_swish = (wanted * normed * gain[...] * (sigma + opened * sigma * (1.0 - sigma))).astype(bf16)
    d_scaled = wanted * (opened * sigma)
    gain_part = jnp.sum(d_scaled * normed, axis=0, keepdims=True)
    d_normed = d_scaled * gain[...]
    d_mixed = root * (d_normed - normed * jnp.mean(d_normed * normed, axis=-1, keepdims=True))
    d_mixed = d_mixed.astype(bf16)
    d_values = mm_tn(scores_in[...], d_mixed).astype(bf16)
    allowed = causal & same_document(seg_row)
    d_scores = jnp.where(allowed, mm_nt(d_mixed, values) * (DK**-0.5), 0.0)
    on_diagonal = jnp.sum(jnp.where(apart == 0, d_scores, 0.0), axis=1, keepdims=True)
    d_query = on_diagonal * keyset
    d_keyset = on_diagonal * query
    both = d_scores + d_scores.T
    exponents = level_exponents(decay)
    d_prefix = d_suffix = d_total = jnp.zeros_like(decay)
    for level, exponent in reversed(list(zip(LEVELS, exponents))):
        upper = bit_of(decay.shape, level)
        if level != LEVELS[-1]:
            d_beside = jnp.where(upper, d_prefix, d_suffix) + d_total
            d_total = d_total + partner(d_beside, level, upper)
        base = jnp.where(upper, query, keyset)
        factor = jnp.exp(exponent)
        scaled = (base * factor).astype(bf16)
        here = jnp.where((apart >= level) & (apart < 2 * level), both, 0.0).astype(bf16)
        d_base = mm(here, scaled) * factor
        d_exponent = d_base * base
        d_query = d_query + jnp.where(upper, d_base, 0.0)
        d_keyset = d_keyset + jnp.where(upper, 0.0, d_base)
        d_prefix = d_prefix + jnp.where(upper, d_exponent, 0.0)
        d_suffix = d_suffix + jnp.where(upper, 0.0, d_exponent)
    d_pre = (d_prefix + d_total) * jax.nn.sigmoid(-pre) * (1.0 / 16.0)
    d_query, d_keyset = d_query.astype(bf16), d_keyset.astype(bf16)
    d_qkvs[:, :DK] = d_query
    d_qkvs[:, DK : 2 * DK] = d_keyset
    d_qkvs[:, 2 * DK : 2 * DK + DV] = d_values
    d_qkvs[:, 2 * DK + DV :] = d_swish
    d_low = lax.dot_general(
        d_pre, up[...], (((1,), (1,)), ((), ())), precision=HIGH, preferred_element_type=f32
    )
    high = d_low.astype(bf16)
    rest = (d_low - high.astype(f32)).astype(bf16)
    d_down[...] += mm_tn(high, first[...]) + mm_tn(rest, first[...])
    d_first[...] = (
        mm_nt(d_query, w_first[:, :DK])
        + mm_nt(d_keyset, w_first[:, DK : 2 * DK])
        + mm_nt(d_values, w_first[:, 2 * DK : 2 * DK + DV])
        + mm_nt(d_swish, w_first[:, 2 * DK + DV :])
        + mm_nt(high, down[...])
        + mm_nt(rest, down[...])
    ).astype(bf16)
    d_up[...] += lax.dot_general(
        low[...], d_pre, (((0,), (0,)), ((), ())), precision=HIGH, preferred_element_type=f32
    )
    d_bias[...] += jnp.sum(d_pre, axis=0, keepdims=True)
    d_gain[...] += gain_part


def dense_forward_kernel(second, w_g, w_u, gate_out, upper_out, product_out):
    gate = mm(second[...], w_g[...])
    gate_out[...] = gate
    upper = mm(second[...], w_u[...])
    upper_out[...] = upper
    product_out[...] = (gate * jax.nn.sigmoid(gate) * upper).astype(bf16)


def dense_backward_kernel(cot, w_d, w_g, w_u, gate_in, upper_in, d_gate_out, d_up_out, d_second):
    gate = gate_in[...]
    sigma = jax.nn.sigmoid(gate)
    d_product = mm(cot[...], w_d[...])
    d_gate = (d_product * upper_in[...] * (sigma + gate * sigma * (1.0 - sigma))).astype(bf16)
    d_up = (d_product * (gate * sigma)).astype(bf16)
    d_gate_out[...] = d_gate
    d_up_out[...] = d_up
    d_second[...] = (mm_nt(d_gate, w_g[...]) + mm_nt(d_up, w_u[...])).astype(bf16)


class Place:
    def __init__(self, sizes):
        self.sizes = sizes
        tall, deep, far, _ = sizes
        place, self.core = lax.axis_index("dp"), lax.axis_index("tensor")
        self.near = place % 2
        self.far_at = (place // 2) % far
        self.y_at = (place // (2 * far)) % deep
        self.z_at = place // (2 * far * deep)
        self.has_above, self.has_below = self.z_at + 1 < tall, self.z_at >= 1
        self.beside = self.device(self.z_at, self.y_at, self.far_at, 1 - self.near, self.core)
        self.other_core = self.device(self.z_at, self.y_at, self.far_at, self.near, 1 - self.core)
        self.above = self.device(self.z_at + 1, self.y_at, self.far_at, self.near, self.core)
        self.below = self.device(self.z_at - 1, self.y_at, self.far_at, self.near, self.core)
        self.shifts = [(fr, yr) for fr in range(far) for yr in range(deep) if fr or yr]

    def device(self, z, y, far_x, near_x, which):
        _, deep, far, _ = self.sizes
        return (((z * deep + y) * far + far_x) * 2 + near_x, which)

    def peer(self, fr, yr):
        _, deep, far, _ = self.sizes
        return self.device(self.z_at, (self.y_at + yr) % deep, (self.far_at + fr) % far, self.near, self.core)

    def block_of(self, slot):
        tall, deep, far, _ = self.sizes
        back_z, back_y, back_far = slot % tall, (slot // tall) % deep, slot // (tall * deep)
        place = (self.z_at + tall - back_z) % tall * deep + (self.y_at + deep - back_y) % deep
        return place * far + (self.far_at + far - back_far) % far

    def greet(self):
        barrier = pltpu.get_barrier_semaphore()

        def signal(who):
            pl.semaphore_signal(barrier, inc=1, device_id=who, device_id_type=pl.DeviceIdType.MESH)

        signal(self.beside)
        signal(self.other_core)
        for fr, yr in self.shifts:
            signal(self.peer(fr, yr))
        tall = self.sizes[0]
        for step_z in range(1, tall):
            signal(self.device((self.z_at + step_z) % tall, self.y_at, self.far_at, self.near, self.core))
        pl.semaphore_wait(barrier, 2 + len(self.shifts) + tall - 1)

    def partners(self):
        tall, deep, far, _ = self.sizes
        found = [self.other_core, self.beside]
        at = (self.z_at, self.y_at, self.far_at)
        for axis, extent in ((2, far), (1, deep), (0, tall)):
            reach = 1
            while reach < extent:
                to = list(at)
                to[axis] = at[axis] + reach - 2 * reach * (at[axis] // reach % 2)
                found.append(self.device(*to, self.near, self.core))
                reach *= 2
        return found


class Copies:
    def __init__(self, send_sem, recv_sem):
        self.send_sem, self.recv_sem, self.used = send_sem, recv_sem, 0

    def make(self, source, target, who):
        index = self.used
        self.used += 1
        return pltpu.make_async_remote_copy(
            src_ref=source, dst_ref=target, send_sem=self.send_sem.at[index], recv_sem=self.recv_sem.at[index],
            device_id=who, device_id_type=pl.DeviceIdType.MESH,
        )


def stream(body, steps, ins, outs):
    pltpu.emit_pipeline(
        body, grid=(steps,),
        in_specs=[pl.BlockSpec(shape, index) for _, shape, index in ins],
        out_specs=[pl.BlockSpec(shape, index) for _, shape, index in outs],
    )(*[one for one, _, _ in ins], *[one for one, _, _ in outs])


def still(i):
    return (0, 0)


def step(i):
    return (i, 0)


def from_tile(first):
    return lambda i: (first + i, 0)


def pull_of(values, gain, wanted):
    root = lax.rsqrt(jnp.mean(values * values, axis=-1, keepdims=True) + norm_eps)
    scaled = wanted * gain
    pulled = root * scaled - values * (root * root * root * jnp.mean(values * scaled, axis=-1, keepdims=True))
    return pulled, jnp.sum(wanted * values * root, axis=0, keepdims=True)


def backward_part(sizes, r, here, copies):
    tall, deep, far, _ = sizes
    core, near, z_at = here.core, here.near, here.z_at
    width = r.cot.shape[1]
    rows = r.cot.shape[0]
    chip_rows = rows // 2
    half_rows = chip_rows // 2
    units = r.product.shape[1]
    tiles = half_rows // 128
    chip_tiles = chip_rows // 256
    outer = deep * far
    size = width // outer // tall
    slab = size * tall
    for total in (r.d_up_acc, r.d_bias_acc, r.d_gain_acc, r.dense_gain_acc, r.mixer_gain_acc, r.d_down_acc):
        total[...] = jnp.zeros_like(total)
    waits = []
    sides = dict(
        d=(r.cot, r.product), g=(r.second, r.d_gate), u=(r.second, r.d_up), f=(r.first, r.d_qkvs),
        o=(r.d_branch, r.gated),
    )
    slab_tile = 256 if slab % 256 == 0 else 128

    def product_slab(group, number, received, target, slabs_of=1):
        left, right = sides[group]
        columns = right.shape[1]
        at = number * slab // slab_tile

        def body(left_ref, right_ref, *rest):
            total = mm_tn(left_ref[...], right_ref[...])
            for other in rest[:-1]:
                total = total + other[...].astype(f32)
            rest[-1][...] = total.astype(bf16)

        stream(
            body, slabs_of * slab // slab_tile,
            [(left, (rows, slab_tile), lambda i: (0, at + i)), (right, (rows, columns), still)]
            + [(one, (slab_tile, columns), step) for one in received],
            [(target, (slab_tile, columns), step)],
        )

    y_copies, z_copies = {}, {}

    def part(ref, index, count):
        return ref.at[pl.ds(index * count, count)]

    def send_slabs(group):
        made = []
        for number in reversed(range(1, outer)):
            fr, yr = number // deep, number % deep
            source, target = (part(getattr(r, name + group), number - 1, slab) for name in ("y_send_", "y_recv_"))
            product_slab(group, number, (), source)
            copy = copies.make(source, target, here.peer((far - fr) % far, (deep - yr) % deep))
            copy.start()
            made.append(copy)
        y_copies[group] = made
        waits.extend(copy.wait_send for copy in made)

    z_first = ("u",)

    def numbers_of(group):
        return range(outer) if group in z_first else (0,)

    def slot_of(group, number, hop, way):
        return (number * (tall - 1) + hop - 1) * 2 + way

    def z_start(group, hop):
        reach = tall - hop
        goes_up, goes_down = z_at + reach < tall, z_at >= reach
        comes_up = here.has_below & (z_at - 1 + reach < tall)
        comes_down = here.has_above & (z_at + 1 >= reach)
        total, sent, received = (getattr(r, name + group) for name in ("sum_", "z_send_", "z_recv_"))
        made = []
        for number in numbers_of(group):
            if hop == 1:
                rising, falling = (part(total, number * tall + at, size) for at in (tall - reach, reach))
            else:
                rising, falling = (part(sent, slot_of(group, number, hop - 1, way), size) for way in (0, 1))
            up = copies.make(rising, part(received, slot_of(group, number, hop, 0), size), here.above)
            down = copies.make(falling, part(received, slot_of(group, number, hop, 1), size), here.below)
            pl.when(goes_up)(up.start)
            pl.when(goes_down)(down.start)
            waits.append(lambda up=up: pl.when(goes_up)(up.wait_send))
            waits.append(lambda down=down: pl.when(goes_down)(down.wait_send))
            made.append((up, down))
        z_copies[group, hop] = made, comes_up, comes_down

    def z_wait(group, hop):
        made, comes_up, comes_down = z_copies[group, hop]
        for up, down in made:
            pl.when(comes_up)(up.wait_recv)
            pl.when(comes_down)(down.wait_recv)

    def own_sum(group):
        for copy in y_copies[group]:
            copy.wait_recv()
        received = getattr(r, "y_recv_" + group)
        product_slab(
            group, 0, [part(received, number - 1, slab) for number in range(1, outer)], getattr(r, "sum_" + group)
        )
        z_start(group, 1)

    def all_slabs(group):
        product_slab(group, 0, (), getattr(r, "sum_" + group), outer)
        z_start(group, 1)

    def z_next(group, hop):
        z_wait(group, hop - 1)
        reach = tall - hop
        total, sent, received = (getattr(r, name + group) for name in ("sum_", "z_send_", "z_recv_"))
        columns = total.shape[1]

        def body(rising, up, falling, down, rising_out, falling_out):
            rising_out[...] = (
                rising[...].astype(f32) + jnp.where(here.has_below, up[...].astype(f32), 0.0)
            ).astype(bf16)
            falling_out[...] = (
                falling[...].astype(f32) + jnp.where(here.has_above, down[...].astype(f32), 0.0)
            ).astype(bf16)

        block = (size, columns)

        def at(index_of):
            return lambda i: (index_of(i), 0)

        stream(
            body, len(numbers_of(group)),
            [
                (total, block, at(lambda i: i * tall + tall - reach)),
                (received, block, at(lambda i: slot_of(group, i, hop - 1, 0))),
                (total, block, at(lambda i: i * tall + reach)),
                (received, block, at(lambda i: slot_of(group, i, hop - 1, 1))),
            ],
            [
                (sent, block, at(lambda i: slot_of(group, i, hop - 1, 0))),
                (sent, block, at(lambda i: slot_of(group, i, hop - 1, 1))),
            ],
        )
        z_start(group, hop)

    def y_last(group):
        z_wait(group, tall - 1)
        total, received, kept = (getattr(r, name + group) for name in ("sum_", "z_recv_", "y_send_"))
        block = (size, total.shape[1])

        def body(own, up, down, into):
            value = own[...].astype(f32) + jnp.where(here.has_below, up[...].astype(f32), 0.0)
            into[...] = (value + jnp.where(here.has_above, down[...].astype(f32), 0.0)).astype(bf16)

        stream(
            body, outer,
            [
                (total, block, lambda i: (i * tall, 0)),
                (received, block, lambda i: (slot_of(group, i, tall - 1, 0), 0)),
                (received, block, lambda i: (slot_of(group, i, tall - 1, 1), 0)),
            ],
            [(kept, block, step)],
        )
        made = []
        for number in range(1, outer):
            fr, yr = number // deep, number % deep
            target = part(getattr(r, "y_recv_" + group), number - 1, size)
            copy = copies.make(
                part(kept, number, size), target, here.peer((far - fr) % far, (deep - yr) % deep)
            )
            copy.start()
            made.append(copy)
        y_copies[group] = made
        waits.extend(copy.wait_send for copy in made)

    def z_finish(group):
        if group in z_first:
            for copy in y_copies[group]:
                copy.wait_recv()
            received = getattr(r, "y_recv_" + group)
            arrays = [part(getattr(r, "y_send_" + group), 0, size)]
            arrays += [part(received, number - 1, size) for number in range(1, outer)]
            counts = [None] * outer
        else:
            z_wait(group, tall - 1)
            received = getattr(r, "z_recv_" + group)
            arrays = [part(getattr(r, "sum_" + group), 0, size)]
            arrays += [part(received, slot_of(group, 0, tall - 1, way), size) for way in (0, 1)]
            counts = [None, here.has_below, here.has_above]
        block = (size // 2, arrays[0].shape[1])
        number_of = len(arrays)

        def body(*both):
            for inputs, into in ((both[:number_of], both[-2]), (both[number_of:-2], both[-1])):
                total = jnp.zeros(block, f32)
                for one, counted in zip(inputs, counts):
                    value = one[...].astype(f32)
                    total = total + (value if counted is None else jnp.where(counted, value, 0.0))
                into[...] = total.astype(into.dtype)

        mine, theirs = (lambda i: (near, 0)), (lambda i: (1 - near, 0))
        crossing = getattr(r, "cross_" + group)
        stream(
            body, 1,
            [(one, block, mine) for one in arrays] + [(one, block, theirs) for one in arrays],
            [(getattr(r, "kept_" + group), block, still), (crossing, block, still)],
        )
        copy = copies.make(crossing, getattr(r, "received_" + group), here.beside)
        copy.start()
        waits.append(copy.wait)

    partners = here.partners()
    exchanges = []

    def small_begin():
        count, _, each = r.by_block.shape
        r.by_block[...] = jnp.zeros_like(r.by_block)
        r.by_head[...] = jnp.zeros_like(r.by_head)
        rank = r.d_up_acc.shape[0]
        for slot in range(count):
            lanes = pl.ds(slot * each, each)
            at = here.block_of(slot)
            r.by_block[at, 0:1, :] = r.mixer_gain_acc[:, lanes]
            r.by_block[at, 1:2, :] = r.dense_gain_acc[:, lanes]
            r.by_block[at, 8 : 8 + rank, :] = r.d_down_acc[:, lanes]
        head = 2 * core + near
        r.by_head[head, 8 : 8 + rank, :] = r.d_up_acc[...]
        r.by_head[head, 0:1, :] = r.d_bias_acc[...]
        r.by_head[0, 1:2, :] = r.d_gain_acc[:, :DK]
        r.by_head[0, 2:3, :] = r.d_gain_acc[:, DK:]

    def small_send():
        index = len(exchanges)
        made = [
            copies.make(own, got.at[index], partners[index])
            for own, got in ((r.by_block, r.got_block), (r.by_head, r.got_head))
        ]
        for copy in made:
            copy.start()
        exchanges.append(made)

    def small_take():
        index = len(exchanges) - 1
        for copy in exchanges[index]:
            copy.wait()
        r.by_block[...] += r.got_block[index]
        r.by_head[...] += r.got_head[index]
        if len(exchanges) < len(partners):
            small_send()
            return True
        return False

    def rows_of(held, start):
        return held.at[pl.ds(pl.multiple_of(start, 128), half_rows)]

    hands, aheads = {}, {}

    def hand(name, following):
        first = (chip_rows if following else 0) + (1 - core) * half_rows
        suffix = "_next" if following else "_own"
        copy = copies.make(rows_of(getattr(r, name), first), getattr(r, "hand_" + name + suffix), here.other_core)
        copy.start()
        hands[name, following] = copy
        waits.append(copy.wait_send)

    def ahead(name):
        hands[name, True].wait_recv()

        def body(one, other, out):
            out[...] = (one[...].astype(f32) + other[...].astype(f32)).astype(bf16)

        block = (128, width)
        stream(
            body, tiles,
            [(getattr(r, name), block, from_tile(2 * tiles + core * tiles)), (getattr(r, "hand_" + name + "_next"), block, step)],
            [(getattr(r, "ahead_" + name), block, step)],
        )
        copy = copies.make(getattr(r, "ahead_" + name), getattr(r, "behind_" + name), here.beside)
        copy.start()
        aheads[name] = copy
        waits.append(copy.wait_send)

    def summed_inputs(name):
        hands[name, False].wait_recv()
        aheads[name].wait_recv()
        block = (128, width)
        return [
            (getattr(r, name), block, from_tile(core * tiles)), (getattr(r, "hand_" + name + "_own"), block, step),
            (getattr(r, "behind_" + name), block, step),
        ]

    def total_of(one, two, three):
        return one[...].astype(f32) + two[...].astype(f32) + three[...].astype(f32)

    def dense_back(first_tile):
        def body(cot, gate, upper, d_gate, d_up, d_second):
            dense_backward_kernel(
                cot, r.v_w_d, r.v_w_g, r.v_w_u, gate, upper, d_gate, d_up, d_second
            )

        at = from_tile(first_tile)
        stream(
            body, chip_tiles,
            [(r.cot, (256, width), at), (r.gate, (256, units), at), (r.upper, (256, units), at)],
            [(r.d_gate, (256, units), at), (r.d_up, (256, units), at), (r.d_second, (256, width), at)],
        )

    def mixer_back(first_tile):
        def body(d_branch, qkv, swish, low, seg_row, scores, mixed, first, d_qkvs, d_first):
            mixer_backward_kernel(
                d_branch, r.v_w_out, r.v_w_first, r.down, qkv, swish, low, seg_row, r.up,
                r.bias, r.gain_heads, scores, mixed, first, d_qkvs, d_first, r.d_up_acc, r.d_bias_acc,
                r.d_gain_acc, r.d_down_acc,
            )

        at = from_tile(first_tile)

        def whole(held):
            return (held, (PIECE, held.shape[1]), at)

        stream(
            body, chip_rows // PIECE,
            [
                whole(r.d_branch), whole(r.qkv), whole(r.swish), whole(r.low),
                (r.seg_row, (1, 1, PIECE), lambda i: (first_tile + i, 0, 0)), whole(r.scores), whole(r.mixed),
                whole(r.first),
            ],
            [whole(r.d_qkvs), whole(r.d_first)],
        )

    block = (128, width)
    own_half = from_tile(core * tiles)

    send_slabs("d")
    yield
    dense_back(chip_tiles)
    hand("d_second", True)
    ahead("d_second")
    dense_back(0)
    hand("d_second", False)
    send_slabs("g")
    all_slabs("u")

    def dense_out_body(product, out):
        out[...] = mm_nt(product[...], r.v_w_d[...]).astype(bf16)

    stream(
        dense_out_body, 2 * chip_tiles, [(r.product, (256, units), step)], [(r.dense, (256, width), step)]
    )

    def hidden_body(one, two, three, cot, hidden, d_hidden, d_branch):
        wanted = total_of(one, two, three)
        pulled, gain_part = pull_of(hidden[...], r.gain_second[...], wanted)
        total = cot[...].astype(f32) + pulled
        d_hidden[...] = total
        d_branch[...] = total.astype(bf16)
        r.dense_gain_acc[...] += gain_part

    stream(
        hidden_body, tiles,
        summed_inputs("d_second") + [(r.cot, block, own_half), (r.hidden, block, step)],
        [(r.d_hidden, block, step), (r.d_branch, block, own_half)],
    )
    mine = rows_of(r.d_branch, core * half_rows)
    there = rows_of(r.d_branch, chip_rows + core * half_rows)
    share_branch = copies.make(mine, mine, here.other_core)
    cross_branch = copies.make(mine, there, here.beside)
    share_branch.start()
    cross_branch.start()
    waits.extend([share_branch.wait_send, cross_branch.wait_send])
    hand("dense", True)
    hand("dense", False)
    share_branch.wait_recv()
    z_next("u", 2)
    mixer_back(0)
    hand("d_first", False)
    cross_branch.wait_recv()
    share_next = copies.make(there, there, here.other_core)
    share_next.start()
    waits.append(share_next.wait_send)
    own_sum("d")
    z_next("u", 3)
    share_next.wait_recv()
    mixer_back(chip_tiles)
    hand("d_first", True)
    send_slabs("f")
    ahead("d_first")
    y_last("u")
    send_slabs("o")
    own_sum("g")
    z_next("d", 2)
    ahead("dense")
    z_next("g", 2)
    z_next("d", 3)

    def tokens_body(one, two, three, d_hidden, tok, out):
        wanted = total_of(one, two, three)
        pulled, gain_part = pull_of(tok[...].astype(f32), r.gain_first[...], wanted)
        out[...] = d_hidden[...] + pulled
        r.mixer_gain_acc[...] += gain_part

    stream(
        tokens_body, tiles,
        summed_inputs("d_first") + [(r.d_hidden, block, step), (r.tok, block, own_half)],
        [(r.grad_tokens, block, own_half)],
    )
    mine = rows_of(r.grad_tokens, core * half_rows)
    copy = copies.make(mine, mine, here.other_core)
    copy.start()
    waits.append(copy.wait)
    small_begin()
    small_send()
    z_next("g", 3)

    def output_body(one, two, three, hidden, out):
        out[...] = (hidden[...] + total_of(one, two, three)).astype(bf16)

    stream(
        output_body, tiles, summed_inputs("dense") + [(r.hidden, block, step)], [(r.output, block, own_half)]
    )
    mine = rows_of(r.output, core * half_rows)
    copy = copies.make(mine, mine, here.other_core)
    copy.start()
    waits.append(copy.wait)
    small_take()
    z_finish("u")
    z_finish("d")
    small_take()
    z_finish("g")
    own_sum("f")
    own_sum("o")
    small_take()
    z_next("f", 2)
    z_next("o", 2)
    small_take()
    z_next("f", 3)
    z_next("o", 3)
    while small_take():
        pass
    z_finish("f")
    z_finish("o")
    yield
    for wait in waits:
        wait()


def forward_part(sizes, r, here, copies):
    tall, deep, far, _ = sizes
    core, near, z_at = here.core, here.near, here.z_at
    first, out, gate, up, down = range(5)
    weights = (r.w_first, r.w_out, r.w_g, r.w_u, r.w_d)
    shards = {
        first: (r.s_query, r.s_key, r.s_value, r.s_swish), out: (r.s_output,), gate: (r.s_gate,), up: (r.s_up,),
        down: (r.s_down,),
    }
    chip_rows, width = r.tokens.shape
    half_rows = chip_rows // 2
    tiles, chip_tiles, pieces = half_rows // 128, chip_rows // 256, chip_rows // PIECE
    outer = deep * far
    block = r.s_query.shape[0]
    size = 2 * block
    units = r.w_g.shape[1]
    waits, locals_made, loads = [], {}, {}

    def local(source, target):
        index = len(locals_made)
        locals_made[index] = copy = pltpu.make_async_copy(source, target, r.load_sem.at[index])
        copy.start()
        return copy

    def load(source, target):
        loads[source] = local(weights[source], target)

    crossings = {}

    def cross(group):
        mine = pl.ds(pl.multiple_of(near * block, 16), block)
        made, at = [], 0
        for shard in shards[group]:
            columns = shard.shape[1] // 2
            there = pl.ds(at, columns)
            keep = shard.at[:, pl.ds(pl.multiple_of(near * columns, 128), columns)]
            give = shard.at[:, pl.ds(pl.multiple_of((1 - near) * columns, 128), columns)]
            target = weights[group].at[mine, there]
            remote = copies.make(give, target, here.beside)
            remote.start()
            made.append((local(keep, target), remote))
            waits.append(remote.wait_send)
            at += columns
        crossings[group] = made

    def arrive(group):
        for kept, remote in crossings[group]:
            kept.wait()
            remote.wait_recv()

    def slab(group, number, back):
        return weights[group].at[pl.ds((number * tall + back) * size, size)]

    sideways = {}

    def spread(group, back, condition=None):
        for number, (fr, yr) in enumerate(here.shifts):
            key = (group, number, back)
            if key not in sideways:
                sideways[key] = copies.make(
                    slab(group, 0, back), slab(group, number + 1, back), here.peer(fr, yr)
                )
            if condition is None:
                sideways[key].start()
            else:
                pl.when(condition)(sideways[key].start)

    def sides_done(group, backs):
        for number in range(outer - 1):
            for back in backs:
                sideways[group, number, back].wait()

    along = {}

    def hop_start(group, hop, numbers=(0,)):
        rises, falls = here.has_above & (z_at >= hop - 1), here.has_below & (z_at + hop - 1 < tall)
        made = []
        for number in numbers:
            rising = copies.make(slab(group, number, hop - 1), slab(group, number, hop), here.above)
            falling = copies.make(
                slab(group, number, (tall - hop + 1) % tall), slab(group, number, tall - hop), here.below
            )
            pl.when(rises)(rising.start)
            pl.when(falls)(falling.start)
            waits.append(lambda rising=rising: pl.when(rises)(rising.wait_send))
            waits.append(lambda falling=falling: pl.when(falls)(falling.wait_send))
            made.append((rising, falling))
        along[group, hop] = made

    def hop_take(group, hop, sideways_too=True, numbers=(0,)):
        came_up, came_down = z_at >= hop, z_at + hop < tall
        for rising, falling in along[group, hop]:
            pl.when(came_up)(rising.wait_recv)
            pl.when(came_down)(falling.wait_recv)
        if hop + 1 < tall:
            hop_start(group, hop + 1, numbers)
        if sideways_too:
            spread(group, hop, came_up)
            spread(group, tall - hop, came_down)

    def rows_of(rows, start):
        return rows.at[pl.ds(pl.multiple_of(start, 128), half_rows)]

    def give_rows(held):
        copy = copies.make(
            rows_of(held, core * half_rows), rows_of(held, chip_rows + core * half_rows), here.beside
        )
        copy.start()
        waits.append(copy.wait_send)
        return copy

    def share_rows(held, start):
        rows = rows_of(held, start + core * half_rows)
        copy = copies.make(rows, rows, here.other_core)
        copy.start()
        waits.append(copy.wait_send)
        return copy

    def reordered(source, target):
        count = outer * tall
        each = width // count

        def body(one, into):
            for slot in range(count):
                place = here.block_of(slot)
                held = one[:, pl.ds(pl.multiple_of(place * each, each), each)] if each % 128 == 0 else None
                into[:, slot * each : (slot + 1) * each] = (
                    one[:, slot * each : (slot + 1) * each] if held is None else held
                )

        stream(
            body, chip_rows // 128, [(source, (128, width), step)], [(target, (128, width), step)]
        )

    def mixer(first_tile):
        def body(tok, seg_row, first_out, low, qkv, swish, scores, mixed, gated):
            mixer_forward_kernel(
                tok, r.v_w_first, r.down, r.gain_first, seg_row, r.up, r.bias, r.gain_heads,
                first_out, low, qkv, swish, scores, mixed, gated,
            )

        at = from_tile(first_tile)

        def whole(held):
            return (held, (PIECE, held.shape[1]), at)

        stream(
            body, pieces, [whole(r.tok), (r.seg_row, (1, 1, PIECE), lambda i: (first_tile + i, 0, 0))],
            [whole(held) for held in (r.first, r.low, r.qkv, r.swish, r.scores, r.mixed, r.gated)],
        )

    def branch_product(first_tile):
        def body(gated, into):
            into[...] = mm_nt(gated[...], r.v_w_out[...]).astype(bf16)

        at = from_tile(first_tile)
        stream(body, chip_tiles, [(r.gated, (256, DV), at)], [(r.branch, (256, width), at)])

    def hand(following):
        start = (chip_rows if following else 0) + (1 - core) * half_rows
        target = r.hand_next if following else r.hand_own
        copy = copies.make(rows_of(r.branch, start), target, here.other_core)
        copy.start()
        waits.append(copy.wait_send)
        return copy

    def dense(first_tile):
        def body(second, gate_out, upper, product):
            dense_forward_kernel(second, r.v_w_g, r.v_w_u, gate_out, upper, product)

        at = from_tile(first_tile)
        stream(
            body, chip_tiles, [(r.second, (256, width), at)],
            [(held, (256, units), at) for held in (r.gate, r.upper, r.product)],
        )

    row_block = (128, width)
    own_half = from_tile(core * tiles)
    everywhere = range(outer)

    cross(first)
    reordered(r.tokens, r.tok)
    seg_own = local(r.seg_in, r.seg_row.at[pl.ds(0, pieces)])
    arrive(first)
    hop_start(first, 1)
    spread(first, 0)
    for group in (out, gate, up, down):
        cross(group)
    seg_cross = copies.make(r.seg_in, r.seg_row.at[pl.ds(pieces, pieces)], here.beside)
    seg_cross.start()
    waits.append(seg_cross.wait_send)
    tok_cross = give_rows(r.tok)
    reordered(r.cotangent, r.cot)
    cot_cross = give_rows(r.cot)
    arrive(out)
    spread(out, 0)
    hop_take(first, 1)
    hop_take(first, 2) if tall > 2 else None
    hop_start(out, 1)
    arrive(gate)
    spread(gate, 0)
    for hop in range(3, tall):
        hop_take(first, hop)
    hop_start(gate, 1)
    tok_cross.wait_recv()
    tok_share = share_rows(r.tok, chip_rows)
    for hop in range(1, tall):
        hop_take(out, hop)
    arrive(up)
    arrive(down)
    sides_done(first, range(tall))
    load(first, r.v_w_first)
    spread(down, 0)
    spread(up, 0)
    seg_own.wait()
    seg_cross.wait_recv()
    tok_share.wait_recv()
    loads[first].wait()
    hop_take(gate, 1)
    mixer(pieces)
    hop_take(gate, 2) if tall > 2 else None
    sides_done(out, range(tall))
    load(out, r.v_w_out)
    hop_start(up, 1)
    loads[out].wait()
    branch_product(chip_tiles)
    hand_next = hand(True)
    mixer(0)
    for hop in range(3, tall):
        hop_take(gate, hop)
    hop_take(up, 1)
    branch_product(0)
    hand_own = hand(False)
    hand_next.wait_recv()

    def ahead_body(one, other, into):
        into[...] = (one[...].astype(f32) + other[...].astype(f32)).astype(bf16)

    stream(
        ahead_body, tiles,
        [(r.branch, row_block, from_tile(2 * tiles + core * tiles)), (r.hand_next, row_block, step)],
        [(r.ahead, row_block, step)],
    )
    ahead = copies.make(r.ahead, r.behind, here.beside)
    ahead.start()
    waits.append(ahead.wait_send)
    cot_cross.wait_recv()
    cot_share = share_rows(r.cot, chip_rows)
    for hop in range(2, tall):
        hop_take(up, hop)
    sides_done(down, (0,))
    hop_start(down, 1, everywhere)
    hand_own.wait_recv()
    ahead.wait_recv()

    def hidden_body(one, two, three, tok, hidden_out, second_out):
        hidden = tok[...].astype(f32) + (
            one[...].astype(f32) + two[...].astype(f32) + three[...].astype(f32)
        )
        hidden_out[...] = hidden
        root = lax.rsqrt(jnp.mean(hidden * hidden, axis=-1, keepdims=True) + norm_eps)
        second_out[...] = (hidden * root * r.gain_second[...]).astype(bf16)

    stream(
        hidden_body, tiles,
        [
            (r.branch, row_block, own_half), (r.hand_own, row_block, step), (r.behind, row_block, step),
            (r.tok, row_block, own_half),
        ],
        [(r.hidden, row_block, step), (r.second, row_block, own_half)],
    )
    second_share = share_rows(r.second, 0)
    second_cross = give_rows(r.second)
    sides_done(gate, range(tall))
    load(gate, r.v_w_g)
    second_cross.wait_recv()
    second_next = share_rows(r.second, chip_rows)
    hop_take(down, 1, False, everywhere)
    sides_done(up, range(tall))
    load(up, r.v_w_u)
    second_share.wait_recv()
    loads[gate].wait()
    loads[up].wait()
    dense(0)
    if tall > 2:
        hop_take(down, 2, False, everywhere)
    second_next.wait_recv()
    dense(chip_tiles)
    cot_share.wait_recv()
    yield
    for hop in range(3, tall):
        hop_take(down, hop, False, everywhere)
    load(down, r.v_w_d)
    loads[down].wait()
    yield
    for wait in waits:
        wait()


def layer_kernel(sizes, names, *refs):
    r = SimpleNamespace(**dict(zip(names, refs)))
    here = Place(sizes)
    here.greet()
    copies = Copies(r.send_sem, r.recv_sem)
    fore, back = forward_part(sizes, r, here, copies), backward_part(sizes, r, here, copies)
    next(fore)
    next(back)
    next(fore)
    next(back)
    for part in (fore, back):
        for _ in part:
            pass


def layer(sizes, small, large):
    tall, deep, far, _ = sizes
    chip_rows, width = large["tokens"].shape
    rows, half_rows = 2 * chip_rows, chip_rows // 2
    pieces = rows // PIECE
    units = large["s_gate"].shape[1] // 2
    rank = small["down"].shape[1]
    qkvs = 2 * DK + 2 * DV
    outer = deep * far
    count = outer * tall
    size = width // count
    slab = size * tall
    outs = dict(
        w_first=(width, qkvs), w_out=(width, DV), w_g=(width, units), w_u=(width, units), w_d=(width, units),
        tok=(rows, width), cot=(rows, width), first=(rows, width), low=(rows, rank, f32), qkv=(rows, 2 * DK + DV),
        swish=(rows, DV, f32), scores=(rows, PIECE), mixed=(rows, DV, f32), gated=(rows, DV),
        hidden=(half_rows, width, f32), second=(rows, width), gate=(rows, units, f32), upper=(rows, units, f32),
        product=(rows, units), branch=(rows, width), hand_next=(half_rows, width), hand_own=(half_rows, width),
        ahead=(half_rows, width), behind=(half_rows, width), d_gate=(rows, units), d_up=(rows, units),
        d_qkvs=(rows, qkvs), d_branch=(rows, width), d_hidden=(half_rows, width, f32), d_second=(rows, width),
        dense=(rows, width), d_first=(rows, width), grad_tokens=(chip_rows, width, f32), output=(chip_rows, width),
    )
    for name in ("d_second", "dense", "d_first"):
        for kind in ("hand_" + name + "_next", "hand_" + name + "_own", "ahead_" + name, "behind_" + name):
            outs[kind] = (half_rows, width)
    for group, columns in dict(d=units, g=units, u=units, f=qkvs, o=DV).items():
        numbers = outer if group == "u" else 1
        outs["kept_" + group] = (size // 2, columns, f32)
        outs["received_" + group] = outs["cross_" + group] = (size // 2, columns)
        outs["sum_" + group] = (numbers * slab, columns)
        outs["y_send_" + group] = (outer * size if group == "u" else (outer - 1) * slab, columns)
        outs["y_recv_" + group] = ((outer - 1) * (size if group == "u" else slab), columns)
        outs["z_send_" + group] = outs["z_recv_" + group] = (numbers * 2 * (tall - 1) * size, columns)
    shapes = {
        name: jax.ShapeDtypeStruct(one[:2], one[2] if len(one) > 2 else bf16) for name, one in outs.items()
    }
    shapes.update(seg_row=jax.ShapeDtypeStruct((pieces, 1, PIECE), jnp.int32))
    heads = large["s_query"].shape[1] * 2 // DK
    inner = dict(
        by_block=jax.ShapeDtypeStruct((count, 8 + rank, size), f32),
        by_head=jax.ShapeDtypeStruct((heads, 8 + rank, DK), f32),
    )
    steps = 2 + int(np.log2(count))
    vmem = pltpu.VMEM
    scratch = dict(
        d_up_acc=vmem((rank, DK), f32), d_bias_acc=vmem((1, DK), f32), d_gain_acc=vmem((1, DV), f32),
        dense_gain_acc=vmem((1, width), f32), mixer_gain_acc=vmem((1, width), f32),
        d_down_acc=vmem((rank, width), f32), got_block=vmem((steps, count, 8 + rank, size), f32),
        got_head=vmem((steps, heads, 8 + rank, DK), f32),
        v_w_first=vmem((width, qkvs), bf16), v_w_out=vmem((width, DV), bf16), v_w_g=vmem((width, units), bf16),
        v_w_u=vmem((width, units), bf16), v_w_d=vmem((width, units), bf16),
    )
    transfers = 8 + 5 * (outer - 1) * tall + (4 + outer) * 2 * (tall - 1) + 12
    transfers += 5 * (outer - 1 + 1) + (4 + outer) * 2 * (tall - 1) + 16 + 2 * steps
    scratch.update(
        load_sem=pltpu.SemaphoreType.DMA((15,)), send_sem=pltpu.SemaphoreType.DMA((transfers,)),
        recv_sem=pltpu.SemaphoreType.DMA((transfers,)),
    )
    anywhere, inside = pl.BlockSpec(memory_space=pl.ANY), pl.BlockSpec(memory_space=vmem)
    names = (*small, *large, *shapes, *inner, *scratch)
    results = pl.pallas_call(
        partial(layer_kernel, sizes, names),
        in_specs=[inside] * len(small) + [anywhere] * len(large),
        out_specs=[anywhere] * len(shapes) + [inside] * len(inner),
        out_shape=[*shapes.values(), *inner.values()],
        scratch_shapes=list(scratch.values()),
        compiler_params=pltpu.CompilerParams(
            collective_id=0, has_side_effects=True, vmem_limit_bytes=vmem_limit
        ),
        cost_estimate=pl.CostEstimate(flops=1, bytes_accessed=1, transcendentals=0),
        name="layer",
    )(*small.values(), *large.values())
    return SimpleNamespace(**dict(zip((*shapes, *inner), results)))


def on_device(
    tokens, segment_ids, cotangent, mixer_gain, w_query, w_key, w_value, w_swish, decay_down, decay_up,
    decay_bias, head_gain, w_output, dense_gain, w_gate, w_up, w_down,
):
    sizes = layout(lax.axis_size("dp"))
    tall, deep, far, _ = sizes
    core = lax.axis_index("tensor")
    place = lax.axis_index("dp")
    z_at, y_at, far_at, near = split_place(place, sizes)
    own_rows = tokens.shape[0]
    half_rows = own_rows // 2
    width = tokens.shape[1]
    block = width // lax.axis_size("dp")

    count = tall * deep * far
    slot = np.arange(count, dtype=np.int32)
    slot_z, slot_y, slot_far = slot % tall, (slot // tall) % deep, slot // (tall * deep)
    from_z, from_y, from_far = slot // (deep * far), (slot // far) % deep, slot % far

    def counted(at, backwards, size):
        return lax.rem(at + (size - backwards), np.int32(size))

    places = (counted(z_at, slot_z, tall) * deep + counted(y_at, slot_y, deep)) * far + counted(far_at, slot_far, far)
    back = (counted(far_at, from_far, far) * deep + counted(y_at, from_y, deep)) * tall + counted(z_at, from_z, tall)

    def blocks_of(values, order):
        chosen = (order[:, None] == slot[None, :]).astype(f32)
        flat = values.astype(f32).reshape(count, -1)
        return jnp.dot(chosen, flat, precision=HIGH).reshape(values.shape)

    def columns(parts, begin, end):
        own, received = (part[:, begin:end].astype(f32) for part in parts)
        return jnp.where(
            near == 0, jnp.concatenate([own, received], 1), jnp.concatenate([received, own], 1)
        )

    gain_first = blocks_of(mixer_gain.astype(f32), places)[None]
    gain_second = blocks_of(dense_gain.astype(f32), places)[None]
    down = blocks_of(decay_down, places).astype(bf16)
    head = 2 * core + near
    up_own = lax.dynamic_slice_in_dim(decay_up, head * DK, DK, 1).astype(f32)
    bias_own = lax.dynamic_slice_in_dim(decay_bias, head * DK, DK, 0).astype(f32)[None]
    gain_heads = head_gain.astype(f32)[None]

    aligned = (width // count) % 128 == 0
    small = dict(
        up=up_own, bias=bias_own, gain_heads=gain_heads, gain_first=gain_first, gain_second=gain_second, down=down
    )
    made = layer(sizes, small, dict(
        tokens=tokens if aligned else reorder(tokens, places),
        cotangent=cotangent if aligned else reorder(cotangent, places),
        seg_in=segment_ids.reshape(own_rows // PIECE, 1, PIECE), s_query=w_query, s_key=w_key, s_value=w_value,
        s_swish=w_swish, s_output=w_output.T, s_gate=w_gate, s_up=w_up, s_down=w_down.T,
    ))
    output = reorder(made.output, back)
    grad_tokens = reorder(made.grad_tokens, back)
    rank = decay_down.shape[1]
    grad_down = made.by_block[:, 8:].transpose(0, 2, 1).reshape(width, rank)
    small = (
        made.by_block[:, 0].reshape(width), made.by_block[:, 1].reshape(width), made.by_head[0, 1:3].reshape(DV),
        grad_down, made.by_head[:, 8:].transpose(1, 0, 2).reshape(rank, -1), made.by_head[:, 0].reshape(-1),
    )
    out_first, out_o, out_g, out_u, out_d = (
        (made.kept_f, made.received_f), (made.kept_o, made.received_o), (made.kept_g, made.received_g),
        (made.kept_u, made.received_u), (made.kept_d, made.received_d),
    )

    def all_of(parts):
        return columns(parts, 0, parts[0].shape[1])

    return (
        output,
        grad_tokens,
        small[0],
        columns(out_first, 0, DK),
        columns(out_first, DK, 2 * DK),
        columns(out_first, 2 * DK, 2 * DK + DV),
        columns(out_first, 2 * DK + DV, 2 * DK + 2 * DV),
        small[3],
        small[4],
        small[5],
        small[2],
        all_of(out_o).T,
        small[1],
        all_of(out_g),
        all_of(out_u),
        all_of(out_d).T,
    )


def solution(mesh):
    rows, large, turned, whole = P("dp", None), P("dp", "tensor"), P("tensor", "dp"), P()
    in_specs = (
        rows, P("dp"), rows, whole, large, large, large, large, whole, whole, whole, whole, turned,
        whole, large, large, turned,
    )
    out_specs = (
        rows, rows, whole, large, large, large, large, whole, whole, whole, whole, turned, whole,
        large, large, turned,
    )
    return jax.shard_map(on_device, mesh=mesh, in_specs=in_specs, out_specs=out_specs, check_vma=False)
```
